512 devices in a mesh: lat: 16 (over y, z_hi, core), head: 32 (over z_lo, x).
Axes of the slice: x: 4, y: 4, z: 16 (z_hi: 2, z_lo: 8; z = z_hi * 8 + z_lo), core: 2. Of those that a mesh axis runs over, the one named last changes fastest.
Arguments:
- hidden: bfloat16 [8192, 5120], P('head', 'lat'), may hold values from -6 to 6
- w_down: bfloat16 [5120, 1536], P('lat', 'head'), may hold values from -0.078125 to 0.078125
- w_up: bfloat16 [1536, 24576], P('head', 'lat'), may hold values from -0.15625 to 0.15625
- norm_gain: float32 [1536], replicated, may hold values from 0.5 to 1.5
- cotangent: bfloat16 [8192, 24576], P('head', 'lat'), may hold values from -6 to 6
Outputs:
- queries: bfloat16 [8192, 24576], P('head', 'lat')
- dhidden: bfloat16 [8192, 5120], P('head', 'lat')
- dgain: float32 [1536], P('lat')
The draws below stay inside these ranges and needn't reach their ends.
All inputs are finite; a program needn't handle non-finite values.
Results may differ from the reference program's by a relative error of at most 0.023.
Values may be sent and summed in bfloat16 or wider, within the bound.
A program may use at most 64 MiB of HBM per device.

```python
import jax
import jax.numpy as jnp
from jax import lax

D = 5120
R = 1536
HQ = 24576
TOKENS = 8192
N_LAT = 16


def block_scale(key, dims, shards, low, top_value):
    def one(dim, blocks):
        heights = jax.random.uniform(jax.random.fold_in(jax.random.fold_in(key, 6), dim), (blocks,), jnp.float32, low / len(shards), top_value / len(shards))
        return jnp.repeat(jnp.exp(heights), dims[dim] // blocks).reshape((-1,) + (1,) * (len(dims) - dim - 1))

    factor_of = one(*shards[0])
    for cut in shards[1:]:
        factor_of = factor_of * one(*cut)
    return factor_of


def gaussian(own_key, dims, width, reach, cuts=(), held_as=jnp.bfloat16):
    loudness = block_scale(own_key, dims, cuts, -0.22, 0.18) if cuts else 1.0
    values = jax.random.normal(own_key, dims, jnp.float32) * width * loudness
    return jnp.minimum(jnp.maximum(values, -reach), reach).astype(held_as)


def setup_inputs(seed: int = 0) -> dict:
    keys = jax.random.split(jax.random.key(seed), 6)
    hidden = gaussian(keys[0], (TOKENS, D), 1.0, 6.0, ((0, 32), (1, 16)))
    w_down = gaussian(keys[1], (D, R), D ** -0.5, 0.078125, ((0, 16), (1, 32)))
    w_up = gaussian(keys[2], (R, HQ), R ** -0.5, 0.15625, ((0, 32), (1, 16)))
    norm_gain = jnp.clip(jax.random.uniform(keys[3], (R,), jnp.float32, 0.5, 1.5), 0.5, 1.5)
    cotangent = gaussian(keys[4], (TOKENS, HQ), 1.0, 6.0, ((0, 32), (1, 16)))
    return dict(hidden=hidden, w_down=w_down, w_up=w_up, norm_gain=norm_gain, cotangent=cotangent)


def reference(hidden, w_down, w_up, norm_gain, cotangent):
    feat_block = D // N_LAT
    col_block = HQ // N_LAT
    hidden_blocks = jnp.moveaxis(hidden.reshape(TOKENS, N_LAT, feat_block), 1, 0)
    down_blocks = w_down.reshape(N_LAT, feat_block, R)

    def add_down(total, pair):
        term = jnp.dot(pair[0], pair[1], preferred_element_type=jnp.float32).astype(jnp.bfloat16)
        term = lax.optimization_barrier(term)
        return (total + term.astype(jnp.float32), None)
    latent, _ = lax.scan(add_down, jnp.zeros((TOKENS, R), jnp.float32), (hidden_blocks, down_blocks))
    scales = lax.rsqrt(lax.optimization_barrier(jnp.sum(latent * latent, axis=1)) / R + 1e-06)
    normed = (latent * scales[:, None] * norm_gain).astype(jnp.bfloat16)
    queries = jnp.dot(normed, w_up, preferred_element_type=jnp.float32).astype(jnp.bfloat16)
    cot_blocks = jnp.moveaxis(cotangent.reshape(TOKENS, N_LAT, col_block), 1, 0)
    up_blocks = jnp.moveaxis(w_up.reshape(R, N_LAT, col_block), 1, 0)

    def add_back(total, pair):
        term = lax.dot_general(pair[0], pair[1], (((1,), (1,)), ((), ())), preferred_element_type=jnp.float32).astype(jnp.bfloat16)
        term = lax.optimization_barrier(term)
        return (total + term.astype(jnp.float32), None)
    dnormed, _ = lax.scan(add_back, jnp.zeros((TOKENS, R), jnp.float32), (cot_blocks, up_blocks))
    weighted = norm_gain * dnormed
    inner_sum = lax.optimization_barrier(jnp.sum(weighted * latent, axis=1))
    dlatent = (scales[:, None] * weighted - latent * (scales ** 3 * inner_sum / R)[:, None]).astype(jnp.bfloat16)
    dhidden = lax.dot_general(dlatent, w_down, (((1,), (1,)), ((), ())), preferred_element_type=jnp.float32).astype(jnp.bfloat16)
    dgain = lax.optimization_barrier(jnp.sum(dnormed * latent * scales[:, None], axis=0))
    return (queries, dhidden, dgain)
```

```python
import jax
import jax.numpy as jnp
from jax import lax
from jax.experimental import pallas as pl
from jax.experimental.pallas import tpu as pltpu
from jax.sharding import PartitionSpec as P

MESH = pl.DeviceIdType.MESH
R = 1536
ROWS = 48
TOK = 256
FEAT = 320
COLS = 1536
CH = 384
F32 = jnp.float32
BF16 = jnp.bfloat16


def kernel(
    hid, wd_in, wu_in, gain, cot,
    q_out, dh_out, dg_out,
    WU, WD, DP, RC, S1, RY, S2, RZ, RES, AG, SC, GS, GR,
    loc, zr, zsu, zsd, xr, xsp, xsm, rel,
    wzr, wzs, wxr, wxp, wxm, wrel,
    cs, cr, ys, yr, hs, hr,
    ahs, ahr, ays, ayr, acs, acr, gs, gr,
):
    lat = lax.axis_index("lat")
    head = lax.axis_index("head")
    x, z = head % 4, head // 4
    y, zh, c = lat // 4, (lat // 2) % 2, lat % 2

    def xdev(d):
        return (lat, z * 4 + (x + d) % 4)

    def zdev(zt):
        return (lat, zt * 4 + x)

    def ydev(d):
        return (((y + d) % 4) * 4 + zh * 2 + c, head)

    cdev = (y * 4 + zh * 2 + (1 - c), head)
    hdev = (y * 4 + (1 - zh) * 2 + c, head)

    def copy(src, dst, ss, rs, dev):
        return pltpu.make_async_remote_copy(
            src_ref=src, dst_ref=dst, send_sem=ss, recv_sem=rs, device_id=dev, device_id_type=MESH
        )

    def send(src, dst, ss, rs, dev):
        copy(src, dst, ss, rs, dev).start()

    def arrived(dst, rs):
        copy(dst, dst, rs, rs, cdev).wait_recv()

    def left(src, ss):
        copy(src, src, ss, ss, cdev).wait_send()

    bar = pltpu.get_barrier_semaphore()
    partners = [xdev(d) for d in (1, 2, 3)] + [ydev(d) for d in (1, 2, 3)] + [cdev, hdev]
    partners += [zdev((z + d) % 8) for d in range(1, 8)]
    for dev in partners:
        pl.semaphore_signal(bar, inc=1, device_id=dev, device_id_type=MESH)
    pl.semaphore_wait(bar, len(partners))

    me = head
    ZORDER = (1, 7, 2, 6, 3, 5, 4)
    for d in ZORDER:
        send(wd_in, WD.at[me], wzs.at[d - 1], wzr.at[z], zdev((z + d) % 8))
    send(wd_in, WD.at[me], wxp.at[z], wxr.at[me], xdev(1))
    send(wd_in, WD.at[me], wxm.at[z], wxr.at[me], xdev(3))
    for k in range(3):
        rows = pl.ds(16 * k, 16)

        @pl.when(z < 7)
        def _():
            send(wu_in.at[rows], WU.at[me, rows], zsu.at[z, k], zr.at[z, k], zdev(jnp.minimum(z + 1, 7)))

        @pl.when(z > 0)
        def _():
            send(wu_in.at[rows], WU.at[me, rows], zsd.at[z, k], zr.at[z, k], zdev(jnp.maximum(z - 1, 0)))

    send(wu_in, WU.at[me], xsp.at[z], xr.at[me], xdev(1))
    send(wu_in, WU.at[me], xsm.at[z], xr.at[me], xdev(3))
    own_u = pltpu.make_async_copy(wu_in, WU.at[me], loc.at[0])
    own_d = pltpu.make_async_copy(wd_in, WD.at[me], loc.at[1])
    own_u.start()
    own_d.start()
    own_u.wait()
    own_d.wait()

    for d in ZORDER:
        zs = (z + d) % 8
        b = zs * 4 + x
        arrived(WD.at[b], wzr.at[zs])
        send(WD.at[b], WD.at[b], wxp.at[zs], wxr.at[b], xdev(1))
        send(WD.at[b], WD.at[b], wxm.at[zs], wxr.at[b], xdev(3))

    def relay_of(zs):
        even = 1 - zs % 2
        from_left, from_right = (x + 3) % 4, (x + 1) % 4
        first = even * from_left + (1 - even) * from_right
        other = even * from_right + (1 - even) * from_left
        return zs * 4 + first, zs * 4 + other, (lat, z * 4 + other)

    def wd_relay(i, _):
        zs = (z + i) % 8
        first, _o, dev = relay_of(zs)
        arrived(WD.at[first], wxr.at[first])
        send(WD.at[first], WD.at[first], wrel.at[zs], wxr.at[first], dev)
        return 0

    def wd_rest(i, _):
        zs = (z + i) % 8
        _f, other, _d = relay_of(zs)
        far = zs * 4 + (x + 2) % 4
        arrived(WD.at[other], wxr.at[other])
        arrived(WD.at[far], wxr.at[far])
        return 0

    def take(zs, up):
        b = zs * 4 + x
        for k in range(3):
            rows = pl.ds(16 * k, 16)
            arrived(WU.at[b, rows], zr.at[zs, k])
            if up:
                @pl.when(z < 7)
                def _():
                    send(WU.at[b, rows], WU.at[b, rows], zsu.at[zs, k], zr.at[zs, k], zdev(jnp.minimum(z + 1, 7)))
            else:
                @pl.when(z > 0)
                def _():
                    send(WU.at[b, rows], WU.at[b, rows], zsd.at[zs, k], zr.at[zs, k], zdev(jnp.maximum(z - 1, 0)))
        send(WU.at[b], WU.at[b], xsp.at[zs], xr.at[b], xdev(1))
        send(WU.at[b], WU.at[b], xsm.at[zs], xr.at[b], xdev(3))

    def both(s, f):
        lo, hi = z - s, z + s

        @pl.when((s >= 0) & (lo >= 0))
        def _():
            f(jnp.maximum(lo, 0), True)

        @pl.when((s >= 1) & (hi <= 7))
        def _():
            f(jnp.minimum(hi, 7), False)

    def relay(zs, up):
        first, _o, dev = relay_of(zs)
        arrived(WU.at[first], xr.at[first])
        send(WU.at[first], WU.at[first], rel.at[zs], xr.at[first], dev)

    def rest(zs, up):
        _f, other, _d = relay_of(zs)
        far = zs * 4 + (x + 2) % 4
        arrived(WU.at[other], xr.at[other])
        arrived(WU.at[far], xr.at[far])

    c_own = pl.ds(pl.multiple_of(c * 128, 128), 128)
    c_other = pl.ds(pl.multiple_of((1 - c) * 128, 128), 128)

    def y_rows(yt):
        return pl.ds(pl.multiple_of(yt * 32, 32), 32)

    h_own = pl.ds(pl.multiple_of(zh * 16, 16), 16)
    h_other = pl.ds(pl.multiple_of((1 - zh) * 16, 16), 16)

    def sum0(j, value):
        DP[j] = value.astype(BF16)
        send(DP.at[j, c_other], RC.at[j], cs.at[j], cr.at[j], cdev)

    def sum1(j):
        arrived(RC.at[j], cr.at[j])
        S1[j] = (DP[j, c_own].astype(F32) + RC[j].astype(F32)).astype(BF16)
        for d in (2, 1, 3):
            send(S1.at[j, y_rows((y + d) % 4)], RY.at[j, d - 1], ys.at[j, d - 1], yr.at[j, d - 1], ydev(d))

    def sum2(j):
        total = S1[j, y_rows(y)].astype(F32)
        for d in (1, 3, 2):
            arrived(RY.at[j, d - 1], yr.at[j, d - 1])
            total = total + RY[j, d - 1].astype(F32)
        S2[j] = total.astype(BF16)
        send(S2.at[j, h_other], RZ.at[j], hs.at[j], hr.at[j], hdev)

    def sum3(j):
        arrived(RZ.at[j], hr.at[j])
        RES[j] = S2[j, h_own].astype(F32) + RZ[j].astype(F32)

    def each(f):
        lax.fori_loop(0, 4, lambda q, v: (f(q), v)[1], 0)

    nt = (((1,), (1,)), ((), ()))

    def down(q):
        w = WD[pl.ds(8 * q, 8)].reshape(CH, FEAT)
        sum0(q, lax.dot_general(hid[...], w, nt, preferred_element_type=F32))

    def up_back(q):
        w = WU[pl.ds(8 * q, 8)].reshape(CH, COLS)
        sum0(4 + q, lax.dot_general(cot[...], w, nt, preferred_element_type=F32))

    def tok(yt, ht):
        return pl.ds(pl.multiple_of(c * 128 + yt * 32 + ht * 16, 16), 16)

    def gather1(k):
        rows = tok(y, zh)
        send(AG.at[k, rows], AG.at[k, rows], ahs.at[k], ahr.at[k], hdev)
        for d in (2, 1, 3):
            send(AG.at[k, rows], AG.at[k, rows], ays.at[k, 0, d - 1], ayr.at[k, 0, d - 1], ydev(d))

    def gather2(k):
        rows = tok(y, 1 - zh)
        arrived(AG.at[k, rows], ahr.at[k])
        for d in (2, 1, 3):
            send(AG.at[k, rows], AG.at[k, rows], ays.at[k, 1, d - 1], ayr.at[k, 1, d - 1], ydev(d))

    def gather3(k):
        for d in (1, 3, 2):
            yt = (y + 4 - d) % 4
            arrived(AG.at[k, tok(yt, zh)], ayr.at[k, 0, d - 1])
            arrived(AG.at[k, tok(yt, 1 - zh)], ayr.at[k, 1, d - 1])
        send(AG.at[k, c_own], AG.at[k, c_own], acs.at[k], acr.at[k], cdev)

    def gather4(k):
        arrived(AG.at[k, c_other], acr.at[k])

    mine = tok(y, zh)

    def norm():
        squares = jnp.zeros((16, 1), F32)
        for q in range(4):
            v = RES[q]
            squares = squares + jnp.sum(v * v, axis=1, keepdims=True)
        scales = lax.rsqrt(squares / R + 1e-06)
        SC[...] = jnp.broadcast_to(scales, (16, 128))
        for q in range(4):
            cols = slice(q * CH, (q + 1) * CH)
            AG[0, mine, cols] = (RES[q] * scales * gain[:, cols]).astype(BF16)

    def back_norm():
        scales = SC[:, 0:1]
        inner = jnp.zeros((16, 1), F32)
        for q in range(4):
            cols = slice(q * CH, (q + 1) * CH)
            inner = inner + jnp.sum(gain[:, cols] * RES[4 + q] * RES[q], axis=1, keepdims=True)
        factor = scales * scales * scales * inner / R
        for q in range(4):
            cols = slice(q * CH, (q + 1) * CH)
            dn, latent = RES[4 + q], RES[q]
            AG[1, mine, cols] = (scales * (gain[:, cols] * dn) - latent * factor).astype(BF16)
            GS[0, :, cols] = jnp.sum(dn * latent * scales, axis=0, keepdims=True)

    def chunk_at(s):
        odd = (s + z) % 2
        q = odd * ((s + z - 1 + 8) // 2 - 4) + (1 - odd) * ((z - s + 16) // 2 - 8)
        ok = (s >= 1) & (q >= 0) & (q <= 3)
        return ok, jnp.clip(q, 0, 3)

    def step(i, carry):
        @pl.when(i <= 6)
        def _():
            s = i + 1
            lo, hi = z - s, z + s

            @pl.when(lo >= 0)
            def _():
                take(jnp.maximum(lo, 0), True)

            @pl.when(hi <= 7)
            def _():
                take(jnp.minimum(hi, 7), False)

        @pl.when(i == 0)
        def _():
            lax.fori_loop(0, 8, wd_relay, 0)

        @pl.when(i == 1)
        def _():
            lax.fori_loop(0, 8, wd_rest, 0)
            each(down)

        both(i - 2, relay)
        both(i - 3, rest)

        @pl.when(i == 2)
        def _():
            each(sum1)

        @pl.when(i == 4)
        def _():
            each(sum2)

        @pl.when(i == 5)
        def _():
            each(sum3)
            norm()
            gather1(0)

        @pl.when(i == 6)
        def _():
            gather2(0)

        @pl.when(i == 8)
        def _():
            gather3(0)

        for lag, f in ((3, sum3), (2, sum2), (1, sum1)):
            ok, q = chunk_at(i - 3 - lag)

            @pl.when(ok)
            def _():
                f(4 + q)

        ok, q = chunk_at(i - 3)

        @pl.when(ok)
        def _():
            up_back(q)

        return carry

    lax.fori_loop(0, 14, step, 0)

    back_norm()
    gather1(1)
    send(GS.at[0], GR.at[0], gs.at[0], gr.at[0], hdev)
    gather4(0)

    def queries(n):
        cols = slice(n * CH, (n + 1) * CH)
        w = WU[:, :, cols].reshape(R, CH)
        q_out[:, cols] = jnp.dot(AG[0], w, preferred_element_type=F32).astype(BF16)

    queries(0)
    queries(1)
    arrived(GR.at[0], gr.at[0])
    GS[1] = GS[0] + GR[0]
    gather2(1)
    for d in (1, 2, 3):
        send(GS.at[1], GR.at[d], gs.at[d], gr.at[d], ydev(d))
    queries(2)
    queries(3)
    total = GS[1]
    for d in (1, 2, 3):
        arrived(GR.at[d], gr.at[d])
        total = total + GR[d]
    GS[2] = total
    gather3(1)
    send(GS.at[2], GR.at[4], gs.at[4], gr.at[4], cdev)
    arrived(GR.at[4], gr.at[4])
    GS[3] = GS[2] + GR[4]
    for d in (1, 2, 3):
        send(GS.at[3], GR.at[4 + d], gs.at[4 + d], gr.at[4 + d], xdev(d))
    gather4(1)
    dh_out[...] = jnp.dot(AG[1], WD[...].reshape(R, FEAT), preferred_element_type=F32).astype(BF16)
    total = GS[3]
    for d in (1, 2, 3):
        arrived(GR.at[4 + d], gr.at[4 + d])
        total = total + GR[4 + d]
    GS[4] = total
    for d in range(1, 8):
        send(GS.at[4], GR.at[7 + d], gs.at[7 + d], gr.at[7 + d], zdev((z + d) % 8))
    for d in range(1, 8):
        arrived(GR.at[7 + d], gr.at[7 + d])
        total = total + GR[7 + d]
    dg_out[...] = total

    for d in range(1, 8):
        left(wd_in, wzs.at[d - 1])
    for zs in range(8):
        left(wd_in, wxp.at[zs])
        left(wd_in, wxm.at[zs])
        left(wd_in, wrel.at[zs])
        left(wu_in, xsp.at[zs])
        left(wu_in, xsm.at[zs])
        left(wu_in, rel.at[zs])
        for k in range(3):
            rows = pl.ds(16 * k, 16)

            @pl.when((zs <= z) & (z < 7))
            def _():
                left(wu_in.at[rows], zsu.at[zs, k])

            @pl.when((zs >= z) & (z > 0))
            def _():
                left(wu_in.at[rows], zsd.at[zs, k])

    def sums_left(j, v):
        left(RC.at[j], cs.at[j])
        for d in range(3):
            left(RY.at[j, d], ys.at[j, d])
        left(RZ.at[j], hs.at[j])
        return v

    lax.fori_loop(0, 8, sums_left, 0)
    for k in range(2):
        left(AG.at[k, mine], ahs.at[k])
        for d in range(3):
            left(AG.at[k, mine], ays.at[k, 0, d])
            left(AG.at[k, mine], ays.at[k, 1, d])
        left(AG.at[k, c_own], acs.at[k])
    for d in range(15):
        left(GS.at[0], gs.at[d])


def body(hidden, w_down, w_up, norm_gain, cotangent):
    vmem = pl.BlockSpec(memory_space=pltpu.VMEM)
    dma = pltpu.SemaphoreType.DMA
    queries, dhidden, dgain = pl.pallas_call(
        kernel,
        name="query_path",
        out_shape=(
            jax.ShapeDtypeStruct((TOK, COLS), BF16),
            jax.ShapeDtypeStruct((TOK, FEAT), BF16),
            jax.ShapeDtypeStruct((1, R), F32),
        ),
        in_specs=[vmem] * 5,
        out_specs=(vmem,) * 3,
        scratch_shapes=[
            pltpu.VMEM((32, ROWS, COLS), BF16),
            pltpu.VMEM((32, ROWS, FEAT), BF16),
            pltpu.VMEM((8, TOK, CH), BF16),
            pltpu.VMEM((8, 128, CH), BF16),
            pltpu.VMEM((8, 128, CH), BF16),
            pltpu.VMEM((8, 3, 32, CH), BF16),
            pltpu.VMEM((8, 32, CH), BF16),
            pltpu.VMEM((8, 16, CH), BF16),
            pltpu.VMEM((8, 16, CH), F32),
            pltpu.VMEM((2, TOK, R), BF16),
            pltpu.VMEM((16, 128), F32),
            pltpu.VMEM((5, 1, R), F32),
            pltpu.VMEM((15, 1, R), F32),
            dma((2,)), dma((8, 3)), dma((8, 3)), dma((8, 3)), dma((32,)), dma((8,)), dma((8,)), dma((8,)),
            dma((8,)), dma((7,)), dma((32,)), dma((8,)), dma((8,)), dma((8,)),
            dma((8,)), dma((8,)), dma((8, 3)), dma((8, 3)), dma((8,)), dma((8,)),
            dma((2,)), dma((2,)), dma((2, 2, 3)), dma((2, 2, 3)), dma((2,)), dma((2,)), dma((15,)), dma((15,)),
        ],
        compiler_params=pltpu.CompilerParams(
            collective_id=0, has_side_effects=True, vmem_limit_bytes=48 * 2**20
        ),
    )(hidden, w_down.T, w_up, norm_gain.reshape(1, R), cotangent)
    share = R // lax.axis_size("lat")
    dgain = lax.dynamic_slice_in_dim(dgain.reshape(R), lax.axis_index("lat") * share, share, 0)
    return queries, dhidden, dgain


def solution(mesh):
    placed = (P("head", "lat"), P("lat", "head"), P("head", "lat"), P(), P("head", "lat"))
    return jax.shard_map(
        body,
        mesh=mesh,
        in_specs=placed,
        out_specs=(P("head", "lat"), P("head", "lat"), P("lat")),
        check_vma=False,
    )
```

```python
import jax
import jax.numpy as jnp
from jax import lax
from jax.experimental import pallas as pl
from jax.experimental.pallas import tpu as pltpu
from jax.sharding import PartitionSpec as P

MESH = pl.DeviceIdType.MESH
R = 1536
ROWS = 48
TOK = 256
FEAT = 320
COLS = 1536
CH = 384
F32 = jnp.float32
BF16 = jnp.bfloat16
NT = (((1,), (1,)), ((), ()))


def unit(n):
    rows, cols = (lax.broadcasted_iota(jnp.int32, (n, n), d) for d in (0, 1))
    return (rows == cols).astype(BF16)


def kernel(
    hid_in, wd_in, wu_in, gain_in, cot_in,
    q_out, dh_out, dg_out,
    hid, hid_v, gain_v, gain, cot, qv,
    WU, WD, DP, RC, S1, RY, S2, RZ, RES, AGN, AGE, DL, SC, IG, INN, GS, GR,
    loc, zr, zsu, zsd, xr, xsp, xsm, rel,
    wzr, wzsu, wzsd, wxr, wxp, wxm, wrel,
    cs, cr, ys, yr, hs, hr,
    ays, ayr, acs, acr, gs, gr,
):
    lat = lax.axis_index("lat")
    head = lax.axis_index("head")
    x, z = head % 4, head // 4
    y, zh, c = lat // 4, (lat // 2) % 2, lat % 2

    def xdev(d):
        return (lat, z * 4 + (x + d) % 4)

    def zdev(zt):
        return (lat, zt * 4 + x)

    def ydev(d, core=c):
        return (((y + d) % 4) * 4 + zh * 2 + core, head)

    cdev = (y * 4 + zh * 2 + (1 - c), head)
    hdev = (y * 4 + (1 - zh) * 2 + c, head)
    group = [ydev(1), ydev(2), ydev(3), cdev, ydev(1, 1 - c), ydev(2, 1 - c), ydev(3, 1 - c)]

    def copy(src, dst, ss, rs, dev):
        return pltpu.make_async_remote_copy(
            src_ref=src, dst_ref=dst, send_sem=ss, recv_sem=rs, device_id=dev, device_id_type=MESH
        )

    def send(src, dst, ss, rs, dev):
        copy(src, dst, ss, rs, dev).start()

    def arrived(dst, rs):
        copy(dst, dst, rs, rs, cdev).wait_recv()

    def left(src, ss):
        copy(src, src, ss, ss, cdev).wait_send()

    bar = pltpu.get_barrier_semaphore()
    partners = [xdev(d) for d in (1, 2, 3)] + group + [hdev]
    partners += [zdev((z + d) % 8) for d in range(1, 8)]
    for dev in partners:
        pl.semaphore_signal(bar, inc=1, device_id=dev, device_id_type=MESH)
    me = head
    inputs = [
        pltpu.make_async_copy(src, dst, loc.at[n])
        for n, (src, dst) in enumerate(
            ((wd_in, WD.at[me]), (wu_in, WU.at[me]), (hid_in, hid_v), (gain_in, gain_v), (cot_in, cot))
        )
    ]
    for cp in inputs:
        cp.start()
    for cp in inputs:
        cp.wait()
    hid[...] = lax.dot_general(unit(TOK), hid_v[...], NT, preferred_element_type=F32).astype(BF16)
    gain[...] = gain_v[...].reshape(1, R)
    IG[...] = 1.0 / gain[...]
    INN[...] = jnp.zeros_like(INN)
    pl.semaphore_wait(bar, len(partners))

    def pass_up(zs, b, rows, k):
        @pl.when(z < 7)
        def _():
            send(WU.at[b, rows], WU.at[b, rows], zsu.at[zs, k], zr.at[zs, k], zdev(jnp.minimum(z + 1, 7)))

    def pass_down(zs, b, rows, k):
        @pl.when(z > 0)
        def _():
            send(WU.at[b, rows], WU.at[b, rows], zsd.at[zs, k], zr.at[zs, k], zdev(jnp.maximum(z - 1, 0)))

    def wd_up(zs, b):
        @pl.when(z < 7)
        def _():
            send(WD.at[b], WD.at[b], wzsu.at[zs], wzr.at[zs], zdev(jnp.minimum(z + 1, 7)))

    def wd_down(zs, b):
        @pl.when(z > 0)
        def _():
            send(WD.at[b], WD.at[b], wzsd.at[zs], wzr.at[zs], zdev(jnp.maximum(z - 1, 0)))

    wd_up(z, me)
    wd_down(z, me)
    for k in range(3):
        pass_up(z, me, pl.ds(16 * k, 16), k)
        pass_down(z, me, pl.ds(16 * k, 16), k)

    def spread(zs, b):
        send(WU.at[b], WU.at[b], xsp.at[zs], xr.at[b], xdev(1))
        send(WU.at[b], WU.at[b], xsm.at[zs], xr.at[b], xdev(3))

    def wd_spread(zs, b):
        send(WD.at[b], WD.at[b], wxp.at[zs], wxr.at[b], xdev(1))
        send(WD.at[b], WD.at[b], wxm.at[zs], wxr.at[b], xdev(3))

    wd_spread(z, me)
    spread(z, me)

    def both(s, f):
        lo, hi = z - s, z + s

        @pl.when((s >= 0) & (lo >= 0))
        def _():
            f(jnp.clip(lo, 0, 7), True)

        @pl.when((s >= 1) & (hi <= 7))
        def _():
            f(jnp.clip(hi, 0, 7), False)

    def relay_of(zs):
        even = 1 - zs % 2
        from_left, from_right = (x + 3) % 4, (x + 1) % 4
        first = even * from_left + (1 - even) * from_right
        other = even * from_right + (1 - even) * from_left
        return zs * 4 + first, zs * 4 + other, (lat, z * 4 + other)

    def wd_take(zs, up):
        b = zs * 4 + x
        arrived(WD.at[b], wzr.at[zs])
        (wd_up if up else wd_down)(zs, b)
        wd_spread(zs, b)

    def wd_relay(zs):
        first, _o, dev = relay_of(zs)
        arrived(WD.at[first], wxr.at[first])
        send(WD.at[first], WD.at[first], wrel.at[zs], wxr.at[first], dev)

    def wd_rest(zs):
        _f, other, _d = relay_of(zs)
        far = zs * 4 + (x + 2) % 4
        arrived(WD.at[other], wxr.at[other])
        arrived(WD.at[far], wxr.at[far])

    def take(zs, up):
        b = zs * 4 + x
        for k in range(3):
            rows = pl.ds(16 * k, 16)
            arrived(WU.at[b, rows], zr.at[zs, k])
            (pass_up if up else pass_down)(zs, b, rows, k)

    def relay(zs):
        first, _o, dev = relay_of(zs)
        arrived(WU.at[first], xr.at[first])
        send(WU.at[first], WU.at[first], rel.at[zs], xr.at[first], dev)

    def rest(zs):
        _f, other, _d = relay_of(zs)
        far = zs * 4 + (x + 2) % 4
        arrived(WU.at[other], xr.at[other])
        arrived(WU.at[far], xr.at[far])

    c_own = pl.ds(pl.multiple_of(c * 128, 128), 128)
    c_other = pl.ds(pl.multiple_of((1 - c) * 128, 128), 128)

    def y_rows(yt):
        return pl.ds(pl.multiple_of(yt * 32, 32), 32)

    def sum0(j, value):
        DP[j] = value.astype(BF16)
        send(DP.at[j, c_other], RC.at[j], cs.at[j], cr.at[j], cdev)

    def sum1(j):
        arrived(RC.at[j], cr.at[j])
        S1[j] = (DP[j, c_own].astype(F32) + RC[j].astype(F32)).astype(BF16)
        for d in (2, 1, 3):
            send(S1.at[j, y_rows((y + d) % 4)], RY.at[j, d - 1], ys.at[j, d - 1], yr.at[j, d - 1], ydev(d))

    def sum2(j):
        total = S1[j, y_rows(y)].astype(F32)
        for d in (1, 3, 2):
            arrived(RY.at[j, d - 1], yr.at[j, d - 1])
            total = total + RY[j, d - 1].astype(F32)
        S2[j] = total.astype(BF16)
        send(S2.at[j], RZ.at[j], hs.at[j], hr.at[j], hdev)

    def sum3(j):
        arrived(RZ.at[j], hr.at[j])
        RES[j] = S2[j].astype(F32) + RZ[j].astype(F32)

    def each(f):
        lax.fori_loop(0, 4, lambda q, v: (f(q), v)[1], 0)

    def down(q):
        w = WD[pl.ds(8 * q, 8)].reshape(CH, FEAT)
        sum0(q, lax.dot_general(hid[...], w, NT, preferred_element_type=F32))

    def up_back(q):
        w = WU[pl.ds(8 * q, 8)].reshape(CH, COLS)
        sum0(4 + q, lax.dot_general(cot[...], w, NT, preferred_element_type=F32))

    def tok(yt):
        return pl.ds(pl.multiple_of(c * 128 + yt * 32, 32), 32)

    mine = tok(y)

    def gather1(m, part):
        for d in (2, 1, 3):
            send(part(mine), part(mine), ays.at[m, d - 1], ayr.at[m, d - 1], ydev(d))

    def gather2(m, part):
        for d in (1, 3, 2):
            arrived(part(tok((y + 4 - d) % 4)), ayr.at[m, d - 1])
        send(part(c_own), part(c_own), acs.at[m], acr.at[m], cdev)

    def gather3(m, part):
        arrived(part(c_other), acr.at[m])

    def fwd(rows):
        return AGN.at[rows]

    def bwd(q):
        return lambda rows: AGE.at[q, rows]

    def norm():
        squares = jnp.zeros((32, 1), F32)
        for q in range(4):
            v = RES[q]
            squares = squares + jnp.sum(v * v, axis=1, keepdims=True)
        scales = lax.rsqrt(squares / R + 1e-06)
        SC[...] = jnp.broadcast_to(scales, (32, 128))
        for q in range(4):
            cols = slice(q * CH, (q + 1) * CH)
            AGN[mine, cols] = (RES[q] * scales * gain[:, cols]).astype(BF16)

    def q_cols(q):
        return pl.ds(pl.multiple_of(q * CH, CH), CH)

    def back3(q):
        sum3(4 + q)
        dn = RES[4 + q]
        scales = SC[:, 0:1]
        AGE[q, mine] = (scales * (gain[:, q_cols(q)] * dn)).astype(BF16)
        gather1(1 + q, bwd(q))
        GS[0, :, q_cols(q)] = jnp.sum(dn * RES[q] * scales, axis=0, keepdims=True)

    def back5(q):
        gather3(1 + q, bwd(q))
        n = AGN[:, q_cols(q)].astype(F32) * IG[:, q_cols(q)]
        part = jnp.sum(AGE[q].astype(F32) * n, axis=1, keepdims=True)
        INN[...] = INN[...] + jnp.broadcast_to(part, (TOK, 128))

    near_z = jnp.minimum(z, 7 - z)
    sign = jnp.where(z < 4, 1, -1)

    def in_turn(n, f):
        two = z + jnp.where(n % 2 == 1, -1, 1) * ((n + 1) // 2)
        one = z + sign * (n - near_z)

        @pl.when((n >= 0) & (n <= 7))
        def _():
            f(jnp.clip(jnp.where(n <= 2 * near_z, two, one), 0, 7))

    def turn(zs):
        d = jnp.abs(zs - z)
        return jnp.where(d > near_z, d + near_z, 2 * d - jnp.where(zs < z, 1, 0))

    def ready(q):
        return jnp.maximum(turn(2 * q), turn(2 * q + 1))

    def queries(n):
        cols = slice(n * CH, (n + 1) * CH)
        w = WU[:, :, cols].reshape(R, CH)
        qv[:, cols] = jnp.dot(AGN[...], w, preferred_element_type=F32).astype(BF16)

    def gain_send(value, slot, dev):
        send(GS.at[value], GR.at[slot], gs.at[slot], gr.at[slot], dev)

    def gain_sum(value, slots):
        total = GS[value]
        for n in slots:
            arrived(GR.at[n], gr.at[n])
            total = total + GR[n]
        return total

    q_copy = pltpu.make_async_copy(qv, q_out, loc.at[5])

    def weights_left():
        for zs in range(8):
            left(WD.at[0], wxp.at[zs])
            left(WD.at[0], wxm.at[zs])
            left(WD.at[0], wrel.at[zs])
            left(WU.at[0], xsp.at[zs])
            left(WU.at[0], xsm.at[zs])
            left(WU.at[0], rel.at[zs])

            @pl.when((zs <= z) & (z < 7))
            def _():
                left(WD.at[0], wzsu.at[zs])
                for k in range(3):
                    left(WU.at[0, pl.ds(16 * k, 16)], zsu.at[zs, k])

            @pl.when((zs >= z) & (z > 0))
            def _():
                left(WD.at[0], wzsd.at[zs])
                for k in range(3):
                    left(WU.at[0, pl.ds(16 * k, 16)], zsd.at[zs, k])

    def sums_left(j, v):
        left(RC.at[j], cs.at[j])
        for d in range(3):
            left(RY.at[j, d], ys.at[j, d])
        left(RZ.at[j], hs.at[j])
        return v

    def done_at(q):
        n = ready(q)
        return 4 + n - jnp.where(n >= 5, 1, 0) - jnp.where(n == 7, 1, 0)

    def step(i, carry):
        def at(when, f, *args):
            @pl.when(i == when)
            def _():
                f(*args)

        def turns(table, f):
            for when, n in table:
                at(when, in_turn, jnp.int32(n), f)

        at(12, weights_left)
        at(14, queries, 0)
        at(14, queries, 1)

        @pl.when(i >= 1)
        def _():
            in_turn(i, lambda zs: spread(zs, zs * 4 + x))

        for when, d in ((0, 2), (1, 3), (2, 4), (3, 5), (3, 6), (4, 7)):
            at(when, both, d, wd_take)
        both(i + 1, take)
        turns(((0, 1), (1, 2), (2, 3), (3, 4), (4, 5), (4, 6), (5, 7)), wd_relay)
        turns(((2, 0), (3, 1), (4, 2), (5, 3), (6, 4), (7, 5), (7, 6), (8, 7)), relay)
        turns(((1, 0), (2, 1), (3, 2), (4, 3), (5, 4)), wd_rest)
        turns(((4, 0), (5, 1), (6, 2), (7, 3), (8, 4), (8, 5), (9, 6), (9, 7)), rest)
        turns(((6, 5), (6, 6), (6, 7)), wd_rest)
        at(6, first)
        at(7, second)
        at(8, third)

        def chunks(stages):
            def chunk(q, v):
                done = done_at(q)
                back = jnp.maximum(done + 3, 11)
                for when, f in stages(done, back):
                    at(when, f, q)
                return v

            lax.fori_loop(0, 4, chunk, 0)

        chunks(lambda done, back: (
            (done + 2, lambda q: sum2(4 + q)),
            (done + 1, lambda q: sum1(4 + q)),
            (done, up_back),
        ))
        at(11, fourth)
        at(12, fifth)
        at(13, sixth)
        chunks(lambda done, back: (
            (back + 2, back5),
            (back + 1, lambda q: gather2(1 + q, bwd(q))),
            (back, back3),
        ))

        @pl.when(i == 12)
        def _():
            for n, dev in enumerate(group):
                gain_send(0, n, dev)

        @pl.when(i == 13)
        def _():
            GS[1] = gain_sum(0, range(7))
            for d in (1, 2, 3):
                gain_send(1, 6 + d, xdev(d))

        return carry

    def first():
        each(down)

    def second():
        each(sum1)

    def third():
        each(sum2)

    def fourth():
        each(sum3)
        norm()
        gather1(0, fwd)

    def fifth():
        gather2(0, fwd)

    def sixth():
        gather3(0, fwd)

    both(1, wd_take)
    in_turn(0, wd_relay)
    lax.fori_loop(0, 15, step, 0)

    inner = INN[:, 0:1] / R
    for q in range(4):
        cols = slice(q * CH, (q + 1) * CH)
        n = AGN[:, cols].astype(F32) * IG[:, cols]
        DL[:, cols] = (AGE[q].astype(F32) - n * inner).astype(BF16)
    dh = jnp.dot(DL[...], WD[...].reshape(R, FEAT), preferred_element_type=F32).astype(BF16)
    dh_out[...] = lax.dot_general(unit(FEAT), dh, NT, preferred_element_type=F32).astype(BF16)
    GS[2] = gain_sum(1, range(7, 10))
    for d in range(1, 8):
        gain_send(2, 9 + d, zdev((z + d) % 8))
    queries(2)
    queries(3)
    q_copy.start()
    lax.fori_loop(0, 8, sums_left, 0)
    dg_out[...] = gain_sum(2, range(10, 17))
    q_copy.wait()

    for m in range(5):
        part = fwd if m == 0 else bwd(m - 1)
        for d in range(3):
            left(part(mine), ays.at[m, d])
        left(part(c_own), acs.at[m])
    for n in range(17):
        left(GS.at[0], gs.at[n])


def body(hidden, w_down, w_up, norm_gain, cotangent):
    vmem = pl.BlockSpec(memory_space=pltpu.VMEM)
    hbm = pl.BlockSpec(memory_space=pltpu.HBM)
    dma = pltpu.SemaphoreType.DMA
    queries, dhidden, dgain = pl.pallas_call(
        kernel,
        name="query_path",
        out_shape=(
            jax.ShapeDtypeStruct((TOK, COLS), BF16),
            jax.ShapeDtypeStruct((FEAT, TOK), BF16),
            jax.ShapeDtypeStruct((1, R), F32),
        ),
        in_specs=[hbm] * 5,
        out_specs=(hbm, vmem, vmem),
        scratch_shapes=[
            pltpu.VMEM((TOK, FEAT), BF16),
            pltpu.VMEM((FEAT, TOK), BF16),
            pltpu.VMEM((R,), F32),
            pltpu.VMEM((1, R), F32),
            pltpu.VMEM((TOK, COLS), BF16),
            pltpu.VMEM((TOK, COLS), BF16),
            pltpu.VMEM((32, ROWS, COLS), BF16),
            pltpu.VMEM((32, ROWS, FEAT), BF16),
            pltpu.VMEM((8, TOK, CH), BF16),
            pltpu.VMEM((8, 128, CH), BF16),
            pltpu.VMEM((8, 128, CH), BF16),
            pltpu.VMEM((8, 3, 32, CH), BF16),
            pltpu.VMEM((8, 32, CH), BF16),
            pltpu.VMEM((8, 32, CH), BF16),
            pltpu.VMEM((8, 32, CH), F32),
            pltpu.VMEM((TOK, R), BF16),
            pltpu.VMEM((4, TOK, CH), BF16),
            pltpu.VMEM((TOK, R), BF16),
            pltpu.VMEM((32, 128), F32),
            pltpu.VMEM((1, R), F32),
            pltpu.VMEM((TOK, 128), F32),
            pltpu.VMEM((3, 1, R), F32),
            pltpu.VMEM((17, 1, R), F32),
            dma((6,)), dma((8, 3)), dma((8, 3)), dma((8, 3)), dma((32,)), dma((8,)), dma((8,)), dma((8,)),
            dma((8,)), dma((8,)), dma((8,)), dma((32,)), dma((8,)), dma((8,)), dma((8,)),
            dma((8,)), dma((8,)), dma((8, 3)), dma((8, 3)), dma((8,)), dma((8,)),
            dma((5, 3)), dma((5, 3)), dma((5,)), dma((5,)), dma((17,)), dma((17,)),
        ],
        compiler_params=pltpu.CompilerParams(
            collective_id=0, has_side_effects=True, vmem_limit_bytes=62 * 2**20
        ),
    )(hidden.T, w_down.T, w_up, norm_gain, cotangent)
    share = R // lax.axis_size("lat")
    dgain = lax.dynamic_slice_in_dim(dgain.reshape(R), lax.axis_index("lat") * share, share, 0)
    return queries, dhidden.T, dgain


def solution(mesh):
    placed = (P("head", "lat"), P("lat", "head"), P("head", "lat"), P(), P("head", "lat"))
    return jax.shard_map(
        body,
        mesh=mesh,
        in_specs=placed,
        out_specs=(P("head", "lat"), P("head", "lat"), P("lat")),
        check_vma=False,
    )
```

```python
import jax
import jax.numpy as jnp
from jax import lax
from jax.experimental import pallas as pl
from jax.experimental.pallas import tpu as pltpu
from jax.sharding import PartitionSpec as P

MESH = pl.DeviceIdType.MESH
R = 1536
ROWS = 48
TOK = 256
FEAT = 320
COLS = 1536
CH = 384
SHARE = 96
F32 = jnp.float32
BF16 = jnp.bfloat16
NT = (((1,), (1,)), ((), ()))


def unit(n):
    rows, cols = (lax.broadcasted_iota(jnp.int32, (n, n), d) for d in (0, 1))
    return (rows == cols).astype(BF16)


def kernel(
    hid_in, wd_in, wu_in, gain_in, cot_in,
    q_out, dh_out, dg_out,
    hid, hid_v, gain_v, gain, cot, qv, dhv,
    WU, WD, DP, RC, S1, RY, S2, RZ, RES, AGN, AGE, DL, SC, IG, INN, GS, GR, GZ,
    loc, zr, zsu, zsd, xr, xsp, xsm, rel,
    wzr, wzsu, wzsd, wxr, wxp, wxm, wrel,
    cs, cr, ys, yr, hs, hr,
    ays, ayr, acs, acr, gs, gr, gzs, gzr,
):
    lat = lax.axis_index("lat")
    head = lax.axis_index("head")
    x, z = head % 4, head // 4
    y, zh, c = lat // 4, (lat // 2) % 2, lat % 2

    def xdev(d):
        return (lat, z * 4 + (x + d) % 4)

    def zdev(zt):
        return (lat, zt * 4 + x)

    def ydev(d):
        return (((y + d) % 4) * 4 + zh * 2 + c, head)

    cdev = (y * 4 + zh * 2 + (1 - c), head)
    hdev = (y * 4 + (1 - zh) * 2 + c, head)
    group = []
    for dx in range(4):
        for dy in range(4):
            for dc in range(2):
                core = c + dc * (1 - 2 * c)
                group.append((((y + dy) % 4) * 4 + zh * 2 + core, z * 4 + (x + dx) % 4))
    group = group[1:]

    def copy(src, dst, ss, rs, dev):
        return pltpu.make_async_remote_copy(
            src_ref=src, dst_ref=dst, send_sem=ss, recv_sem=rs, device_id=dev, device_id_type=MESH
        )

    def send(src, dst, ss, rs, dev):
        copy(src, dst, ss, rs, dev).start()

    def arrived(dst, rs):
        copy(dst, dst, rs, rs, cdev).wait_recv()

    def left(src, ss):
        copy(src, src, ss, ss, cdev).wait_send()

    bar = pltpu.get_barrier_semaphore()
    partners = group + [hdev]
    partners += [zdev((z + d) % 8) for d in range(1, 8)]
    for dev in partners:
        pl.semaphore_signal(bar, inc=1, device_id=dev, device_id_type=MESH)
    me = head
    inputs = [
        pltpu.make_async_copy(src, dst, loc.at[n])
        for n, (src, dst) in enumerate(
            ((wd_in, WD.at[me]), (wu_in, WU.at[me]), (hid_in, hid_v), (gain_in, gain_v), (cot_in, cot))
        )
    ]
    for cp in inputs:
        cp.start()
    for cp in inputs:
        cp.wait()
    hid[...] = lax.dot_general(unit(TOK), hid_v[...], NT, preferred_element_type=F32).astype(BF16)
    gain[...] = gain_v[...].reshape(1, R)
    IG[...] = 1.0 / gain[...]
    INN[...] = jnp.zeros_like(INN)
    pl.semaphore_wait(bar, len(partners))

    def pass_up(zs, b, rows, k):
        @pl.when(z < 7)
        def _():
            send(WU.at[b, rows], WU.at[b, rows], zsu.at[zs, k], zr.at[zs, k], zdev(jnp.minimum(z + 1, 7)))

    def pass_down(zs, b, rows, k):
        @pl.when(z > 0)
        def _():
            send(WU.at[b, rows], WU.at[b, rows], zsd.at[zs, k], zr.at[zs, k], zdev(jnp.maximum(z - 1, 0)))

    def wd_up(zs, b):
        @pl.when(z < 7)
        def _():
            send(WD.at[b], WD.at[b], wzsu.at[zs], wzr.at[zs], zdev(jnp.minimum(z + 1, 7)))

    def wd_down(zs, b):
        @pl.when(z > 0)
        def _():
            send(WD.at[b], WD.at[b], wzsd.at[zs], wzr.at[zs], zdev(jnp.maximum(z - 1, 0)))

    wd_up(z, me)
    wd_down(z, me)
    for k in range(3):
        pass_up(z, me, pl.ds(16 * k, 16), k)
        pass_down(z, me, pl.ds(16 * k, 16), k)

    def spread(zs, b):
        send(WU.at[b], WU.at[b], xsp.at[zs], xr.at[b], xdev(1))
        send(WU.at[b], WU.at[b], xsm.at[zs], xr.at[b], xdev(3))

    def own_spread(zs):
        spread(zs, zs * 4 + x)

    def wd_spread(zs, b):
        send(WD.at[b], WD.at[b], wxp.at[zs], wxr.at[b], xdev(1))
        send(WD.at[b], WD.at[b], wxm.at[zs], wxr.at[b], xdev(3))

    wd_spread(z, me)
    spread(z, me)

    def both(s, f):
        lo, hi = z - s, z + s

        @pl.when((s >= 0) & (lo >= 0))
        def _():
            f(jnp.clip(lo, 0, 7), True)

        @pl.when((s >= 1) & (hi <= 7))
        def _():
            f(jnp.clip(hi, 0, 7), False)

    def relay_of(zs):
        even = 1 - zs % 2
        from_left, from_right = (x + 3) % 4, (x + 1) % 4
        first = even * from_left + (1 - even) * from_right
        other = even * from_right + (1 - even) * from_left
        return zs * 4 + first, zs * 4 + other, (lat, z * 4 + other)

    def wd_take(zs, up):
        b = zs * 4 + x
        arrived(WD.at[b], wzr.at[zs])
        (wd_up if up else wd_down)(zs, b)
        wd_spread(zs, b)

    def wd_relay(zs):
        first, _o, dev = relay_of(zs)
        arrived(WD.at[first], wxr.at[first])
        send(WD.at[first], WD.at[first], wrel.at[zs], wxr.at[first], dev)

    def wd_rest(zs):
        _f, other, _d = relay_of(zs)
        far = zs * 4 + (x + 2) % 4
        arrived(WD.at[other], wxr.at[other])
        arrived(WD.at[far], wxr.at[far])

    def take(zs, up):
        b = zs * 4 + x
        for k in range(3):
            rows = pl.ds(16 * k, 16)
            arrived(WU.at[b, rows], zr.at[zs, k])
            (pass_up if up else pass_down)(zs, b, rows, k)

    def relay(zs):
        first, _o, dev = relay_of(zs)
        arrived(WU.at[first], xr.at[first])
        send(WU.at[first], WU.at[first], rel.at[zs], xr.at[first], dev)

    def rest(zs):
        _f, other, _d = relay_of(zs)
        far = zs * 4 + (x + 2) % 4
        arrived(WU.at[other], xr.at[other])
        arrived(WU.at[far], xr.at[far])

    c_own = pl.ds(pl.multiple_of(c * 128, 128), 128)
    c_other = pl.ds(pl.multiple_of((1 - c) * 128, 128), 128)

    def y_rows(yt):
        return pl.ds(pl.multiple_of(yt * 32, 32), 32)

    def sum0(j, value):
        DP[j] = value.astype(BF16)
        send(DP.at[j, c_other], RC.at[j], cs.at[j], cr.at[j], cdev)

    def sum1(j):
        arrived(RC.at[j], cr.at[j])
        S1[j] = (DP[j, c_own].astype(F32) + RC[j].astype(F32)).astype(BF16)
        for d in (2, 1, 3):
            send(S1.at[j, y_rows((y + d) % 4)], RY.at[j, d - 1], ys.at[j, d - 1], yr.at[j, d - 1], ydev(d))

    def sum2(j):
        total = S1[j, y_rows(y)].astype(F32)
        for d in (1, 3, 2):
            arrived(RY.at[j, d - 1], yr.at[j, d - 1])
            total = total + RY[j, d - 1].astype(F32)
        S2[j] = total.astype(BF16)
        send(S2.at[j], RZ.at[j], hs.at[j], hr.at[j], hdev)

    def sum3(j):
        arrived(RZ.at[j], hr.at[j])
        RES[j] = S2[j].astype(F32) + RZ[j].astype(F32)

    def each(f):
        lax.fori_loop(0, 4, lambda q, v: (f(q), v)[1], 0)

    def down(q):
        w = WD[pl.ds(8 * q, 8)].reshape(CH, FEAT)
        sum0(q, lax.dot_general(hid[...], w, NT, preferred_element_type=F32))

    def up_back(q):
        w = WU[pl.ds(8 * q, 8)].reshape(CH, COLS)
        sum0(4 + q, lax.dot_general(cot[...], w, NT, preferred_element_type=F32))

    def tok(yt):
        return pl.ds(pl.multiple_of(c * 128 + yt * 32, 32), 32)

    mine = tok(y)

    def gather1(m, part):
        for d in (2, 1, 3):
            send(part(mine), part(mine), ays.at[m, d - 1], ayr.at[m, d - 1], ydev(d))

    def gather2(m, part):
        for d in (1, 3, 2):
            arrived(part(tok((y + 4 - d) % 4)), ayr.at[m, d - 1])
        send(part(c_own), part(c_own), acs.at[m], acr.at[m], cdev)

    def gather3(m, part):
        arrived(part(c_other), acr.at[m])

    def fwd(rows):
        return AGN.at[rows]

    def bwd(q):
        return lambda rows: AGE.at[q, rows]

    def norm():
        squares = jnp.zeros((32, 1), F32)
        for q in range(4):
            v = RES[q]
            squares = squares + jnp.sum(v * v, axis=1, keepdims=True)
        scales = lax.rsqrt(squares / R + 1e-06)
        SC[...] = jnp.broadcast_to(scales, (32, 128))
        for q in range(4):
            cols = slice(q * CH, (q + 1) * CH)
            AGN[mine, cols] = (RES[q] * scales * gain[:, cols]).astype(BF16)

    def q_cols(q):
        return pl.ds(pl.multiple_of(q * CH, CH), CH)

    def back3(q):
        sum3(4 + q)
        dn = RES[4 + q]
        scales = SC[:, 0:1]
        AGE[q, mine] = (scales * (gain[:, q_cols(q)] * dn)).astype(BF16)
        gather1(1 + q, bwd(q))
        GS[0, :, q_cols(q)] = jnp.sum(dn * RES[q] * scales, axis=0, keepdims=True)

    def back5(q):
        gather3(1 + q, bwd(q))
        n = AGN[:, q_cols(q)].astype(F32) * IG[:, q_cols(q)]
        part = jnp.sum(AGE[q].astype(F32) * n, axis=1, keepdims=True)
        INN[...] = INN[...] + jnp.broadcast_to(part, (TOK, 128))

    near_z = jnp.minimum(z, 7 - z)
    sign = jnp.where(z < 4, 1, -1)

    def in_turn(n, f):
        two = z + jnp.where(n % 2 == 1, -1, 1) * ((n + 1) // 2)
        one = z + sign * (n - near_z)

        @pl.when((n >= 0) & (n <= 7))
        def _():
            f(jnp.clip(jnp.where(n <= 2 * near_z, two, one), 0, 7))

    def turn(zs):
        d = jnp.abs(zs - z)
        return jnp.where(d > near_z, d + near_z, 2 * d - jnp.where(zs < z, 1, 0))

    def ready(q):
        return jnp.maximum(turn(2 * q), turn(2 * q + 1))

    def queries(n):
        cols = slice(n * CH, (n + 1) * CH)
        w = WU[:, :, cols].reshape(R, CH)
        qv[:, cols] = jnp.dot(AGN[...], w, preferred_element_type=F32).astype(BF16)

    q_copy = pltpu.make_async_copy(qv, q_out, loc.at[5])

    def weights_left():
        for zs in range(8):
            left(WD.at[0], wxp.at[zs])
            left(WD.at[0], wxm.at[zs])
            left(WD.at[0], wrel.at[zs])
            left(WU.at[0], xsp.at[zs])
            left(WU.at[0], xsm.at[zs])
            left(WU.at[0], rel.at[zs])

            @pl.when((zs <= z) & (z < 7))
            def _():
                left(WD.at[0], wzsu.at[zs])
                for k in range(3):
                    left(WU.at[0, pl.ds(16 * k, 16)], zsu.at[zs, k])

            @pl.when((zs >= z) & (z > 0))
            def _():
                left(WD.at[0], wzsd.at[zs])
                for k in range(3):
                    left(WU.at[0, pl.ds(16 * k, 16)], zsd.at[zs, k])

    def sums_left(j, v):
        left(RC.at[j], cs.at[j])
        for d in range(3):
            left(RY.at[j, d], ys.at[j, d])
        left(RZ.at[j], hs.at[j])
        return v

    def done_at(q):
        n = ready(q)
        return 4 + n - jnp.where(n >= 5, 1, 0) - jnp.where(n == 7, 1, 0)

    def run_at(i, when, f, *args):
        @pl.when(i == when)
        def _():
            f(*args)

    def chunks(i, lag, earliest, f):
        def chunk(q, v):
            run_at(i, jnp.maximum(done_at(q) + lag, earliest), f, q)
            return v

        lax.fori_loop(0, 4, chunk, 0)

    def step(i, carry):
        def at(when, f, *args):
            run_at(i, when, f, *args)

        def turns(table, f):
            for when, n in table:
                at(when, in_turn, jnp.int32(n), f)

        turns(((1, 1), (2, 2), (3, 3), (4, 4)), own_spread)
        for when, d in ((0, 2), (1, 3), (2, 4), (3, 5), (3, 6), (4, 7)):
            at(when, both, d, wd_take)
        both(i + 1, take)
        turns(((4, 5),), own_spread)
        turns(((0, 1), (1, 2), (2, 3), (3, 4), (4, 5), (4, 6), (5, 7)), wd_relay)
        turns(((5, 6), (6, 7)), own_spread)
        turns(((2, 0), (3, 1), (4, 2), (5, 3), (6, 4), (6, 5)), relay)
        at(7, second)
        turns(((7, 6), (7, 7)), relay)
        turns(((1, 0), (2, 1), (3, 2), (4, 3), (5, 4)), wd_rest)
        turns(((4, 0), (5, 1), (6, 2), (7, 3), (8, 4), (8, 5)), rest)
        at(8, third)
        turns(((9, 6), (9, 7)), rest)
        turns(((6, 5), (6, 6), (6, 7)), wd_rest)
        at(6, first)
        chunks(i, 0, 0, up_back)
        chunks(i, 1, 0, lambda q: sum1(4 + q))
        chunks(i, 2, 0, lambda q: sum2(4 + q))
        return carry

    def first():
        each(down)

    def second():
        each(sum1)

    def third():
        each(sum2)

    def fourth():
        each(sum3)
        norm()
        gather1(0, fwd)

    def fifth():
        gather2(0, fwd)

    def sixth():
        gather3(0, fwd)

    both(1, wd_take)
    in_turn(0, wd_relay)
    lax.fori_loop(0, 10, step, 0)

    chunks(10, 1, 0, lambda q: sum1(4 + q))
    chunks(10, 2, 0, lambda q: sum2(4 + q))
    weights_left()
    chunks(11, 2, 0, lambda q: sum2(4 + q))
    fourth()
    chunks(11, 3, 11, back3)
    chunks(12, 3, 11, back3)
    for n, dev in enumerate(group):
        send(GS.at[0], GR.at[n], gs.at[n], gr.at[n], dev)
    fifth()
    chunks(12, 4, 12, lambda q: gather2(1 + q, bwd(q)))
    sixth()
    queries(0)
    queries(1)
    chunks(13, 4, 12, lambda q: gather2(1 + q, bwd(q)))
    total = GS[0]
    for n in range(31):
        arrived(GR.at[n], gr.at[n])
        total = total + GR[n]
    GS[1] = total
    for k in range(16):
        @pl.when(lat == k)
        def _():
            GZ[0] = GS[1, :, k * SHARE:(k + 1) * SHARE]

    for d in range(1, 8):
        send(GZ.at[0], GZ.at[d], gzs.at[d - 1], gzr.at[d - 1], zdev((z + d) % 8))
    chunks(13, 5, 13, back5)
    chunks(14, 5, 13, back5)
    inner = INN[:, 0:1] / R
    for q in range(4):
        cols = slice(q * CH, (q + 1) * CH)
        n = AGN[:, cols].astype(F32) * IG[:, cols]
        DL[:, cols] = (AGE[q].astype(F32) - n * inner).astype(BF16)
    dh = jnp.dot(DL[...], WD[...].reshape(R, FEAT), preferred_element_type=F32).astype(BF16)
    dhv[...] = lax.dot_general(unit(FEAT), dh, NT, preferred_element_type=F32).astype(BF16)
    dh_copy = pltpu.make_async_copy(dhv, dh_out, loc.at[0])
    dh_copy.start()
    queries(2)
    queries(3)
    q_copy.start()
    lax.fori_loop(0, 8, sums_left, 0)
    for m in range(5):
        part = fwd if m == 0 else bwd(m - 1)
        for d in range(3):
            left(part(mine), ays.at[m, d])
        left(part(c_own), acs.at[m])
    for n in range(31):
        left(GS.at[0], gs.at[n])
    share = GZ[0]
    for d in range(1, 8):
        arrived(GZ.at[d], gzr.at[d - 1])
        share = share + GZ[d]
    dg_out[...] = share
    for d in range(7):
        left(GZ.at[0], gzs.at[d])
    q_copy.wait()
    dh_copy.wait()


def body(hidden, w_down, w_up, norm_gain, cotangent):
    vmem = pl.BlockSpec(memory_space=pltpu.VMEM)
    hbm = pl.BlockSpec(memory_space=pltpu.HBM)
    dma = pltpu.SemaphoreType.DMA
    queries, dhidden, dgain = pl.pallas_call(
        kernel,
        name="query_path",
        out_shape=(
            jax.ShapeDtypeStruct((TOK, COLS), BF16),
            jax.ShapeDtypeStruct((FEAT, TOK), BF16),
            jax.ShapeDtypeStruct((1, SHARE), F32),
        ),
        in_specs=[hbm] * 5,
        out_specs=(hbm, hbm, vmem),
        scratch_shapes=[
            pltpu.VMEM((TOK, FEAT), BF16),
            pltpu.VMEM((FEAT, TOK), BF16),
            pltpu.VMEM((R,), F32),
            pltpu.VMEM((1, R), F32),
            pltpu.VMEM((TOK, COLS), BF16),
            pltpu.VMEM((TOK, COLS), BF16),
            pltpu.VMEM((FEAT, TOK), BF16),
            pltpu.VMEM((32, ROWS, COLS), BF16),
            pltpu.VMEM((32, ROWS, FEAT), BF16),
            pltpu.VMEM((8, TOK, CH), BF16),
            pltpu.VMEM((8, 128, CH), BF16),
            pltpu.VMEM((8, 128, CH), BF16),
            pltpu.VMEM((8, 3, 32, CH), BF16),
            pltpu.VMEM((8, 32, CH), BF16),
            pltpu.VMEM((8, 32, CH), BF16),
            pltpu.VMEM((8, 32, CH), F32),
            pltpu.VMEM((TOK, R), BF16),
            pltpu.VMEM((4, TOK, CH), BF16),
            pltpu.VMEM((TOK, R), BF16),
            pltpu.VMEM((32, 128), F32),
            pltpu.VMEM((1, R), F32),
            pltpu.VMEM((TOK, 128), F32),
            pltpu.VMEM((2, 1, R), F32),
            pltpu.VMEM((31, 1, R), F32),
            pltpu.VMEM((8, 1, SHARE), F32),
            dma((6,)), dma((8, 3)), dma((8, 3)), dma((8, 3)), dma((32,)), dma((8,)), dma((8,)), dma((8,)),
            dma((8,)), dma((8,)), dma((8,)), dma((32,)), dma((8,)), dma((8,)), dma((8,)),
            dma((8,)), dma((8,)), dma((8, 3)), dma((8, 3)), dma((8,)), dma((8,)),
            dma((5, 3)), dma((5, 3)), dma((5,)), dma((5,)), dma((31,)), dma((31,)), dma((7,)), dma((7,)),
        ],
        compiler_params=pltpu.CompilerParams(
            collective_id=0, has_side_effects=True, vmem_limit_bytes=62 * 2**20
        ),
    )(hidden.T, w_down.T, w_up, norm_gain, cotangent)
    return queries, dhidden.T, dgain.reshape(SHARE)


def solution(mesh):
    placed = (P("head", "lat"), P("lat", "head"), P("head", "lat"), P(), P("head", "lat"))
    return jax.shard_map(
        body,
        mesh=mesh,
        in_specs=placed,
        out_specs=(P("head", "lat"), P("head", "lat"), P("lat")),
        check_vma=False,
    )
```

```python
import jax
import jax.numpy as jnp
from jax import lax
from jax.experimental import pallas as pl
from jax.experimental.pallas import tpu as pltpu
from jax.sharding import PartitionSpec as P

MESH = pl.DeviceIdType.MESH
R = 1536
ROWS = 48
TOK = 256
FEAT = 320
COLS = 1536
CH = 384
SHARE = 96
F32 = jnp.float32
BF16 = jnp.bfloat16
NT = (((1,), (1,)), ((), ()))


def unit(n):
    rows, cols = (lax.broadcasted_iota(jnp.int32, (n, n), d) for d in (0, 1))
    return (rows == cols).astype(BF16)


def kernel(
    hid_in, wd_in, wu_in, gain_in, cot_in,
    q_out, dh_out, dg_out,
    hid, hid_v, gain_v, gain, cot, qv, dhv,
    WU, WD, DP, RC, S1, RY, S2, RZ, RES, AGN, AGE, DL, SC, IG, INN, GS, GR, GZ,
    loc, zr, zs_sem, xr, xs, wzr, wzs, wxr, wxs,
    cs, cr, ys, yr, hs, hr,
    ays, ayr, acs, acr, gs, gr, gzs, gzr,
):
    lat = lax.axis_index("lat")
    head = lax.axis_index("head")
    x, z = head % 4, head // 4
    y, zh, c = lat // 4, (lat // 2) % 2, lat % 2

    def xdev(d):
        return (lat, z * 4 + (x + d) % 4)

    def zdev(zt):
        return (lat, zt * 4 + x)

    def ydev(d):
        return (((y + d) % 4) * 4 + zh * 2 + c, head)

    cdev = (y * 4 + zh * 2 + (1 - c), head)
    hdev = (y * 4 + (1 - zh) * 2 + c, head)
    group = []
    for dx in range(4):
        for dy in range(4):
            for dc in range(2):
                core = c + dc * (1 - 2 * c)
                group.append((((y + dy) % 4) * 4 + zh * 2 + core, z * 4 + (x + dx) % 4))
    group = group[1:]

    def copy(src, dst, ss, rs, dev):
        return pltpu.make_async_remote_copy(
            src_ref=src, dst_ref=dst, send_sem=ss, recv_sem=rs, device_id=dev, device_id_type=MESH
        )

    def send(src, dst, ss, rs, dev):
        copy(src, dst, ss, rs, dev).start()

    def arrived(dst, rs):
        copy(dst, dst, rs, rs, cdev).wait_recv()

    def left(src, ss):
        copy(src, src, ss, ss, cdev).wait_send()

    bar = pltpu.get_barrier_semaphore()
    partners = group + [hdev]
    partners += [zdev((z + d) % 8) for d in range(1, 8)]
    for dev in partners:
        pl.semaphore_signal(bar, inc=1, device_id=dev, device_id_type=MESH)
    me = head
    inputs = [
        pltpu.make_async_copy(src, dst, loc.at[n])
        for n, (src, dst) in enumerate(
            ((wd_in, WD.at[me]), (wu_in, WU.at[me]), (hid_in, hid_v), (gain_in, gain_v), (cot_in, cot))
        )
    ]
    for cp in inputs:
        cp.start()
    for cp in inputs:
        cp.wait()
    hid[...] = lax.dot_general(unit(TOK), hid_v[...], NT, preferred_element_type=F32).astype(BF16)
    gain[...] = gain_v[...].reshape(1, R)
    IG[...] = 1.0 / gain[...]
    INN[...] = jnp.zeros_like(INN)
    pl.semaphore_wait(bar, len(partners))

    def pass_up(zs, b, rows, k):
        @pl.when(z < 7)
        def _():
            send(WU.at[b, rows], WU.at[b, rows], zs_sem, zr.at[zs, k], zdev(jnp.minimum(z + 1, 7)))

    def pass_down(zs, b, rows, k):
        @pl.when(z > 0)
        def _():
            send(WU.at[b, rows], WU.at[b, rows], zs_sem, zr.at[zs, k], zdev(jnp.maximum(z - 1, 0)))

    def wd_up(zs, b):
        @pl.when(z < 7)
        def _():
            send(WD.at[b], WD.at[b], wzs, wzr.at[zs], zdev(jnp.minimum(z + 1, 7)))

    def wd_down(zs, b):
        @pl.when(z > 0)
        def _():
            send(WD.at[b], WD.at[b], wzs, wzr.at[zs], zdev(jnp.maximum(z - 1, 0)))

    wd_up(z, me)
    wd_down(z, me)
    for k in range(3):
        pass_up(z, me, pl.ds(16 * k, 16), k)
        pass_down(z, me, pl.ds(16 * k, 16), k)

    def spread(zs, b):
        even = 1 - zs % 2
        send(WU.at[b], WU.at[b], xs, xr.at[zs + 8 * (1 - even)], xdev(1))
        send(WU.at[b], WU.at[b], xs, xr.at[zs + 8 * even], xdev(3))

    def own_spread(zs):
        spread(zs, zs * 4 + x)

    def wd_spread(zs, b):
        even = 1 - zs % 2
        send(WD.at[b], WD.at[b], wxs, wxr.at[even * zs + 8 * (1 - even)], xdev(1))
        send(WD.at[b], WD.at[b], wxs, wxr.at[(1 - even) * zs + 8 * even], xdev(3))

    wd_spread(z, me)
    spread(z, me)

    def both(s, f):
        lo, hi = z - s, z + s

        @pl.when((s >= 0) & (lo >= 0))
        def _():
            f(jnp.clip(lo, 0, 7), True)

        @pl.when((s >= 1) & (hi <= 7))
        def _():
            f(jnp.clip(hi, 0, 7), False)

    def relay_of(zs):
        even = 1 - zs % 2
        from_left, from_right = (x + 3) % 4, (x + 1) % 4
        first = even * from_left + (1 - even) * from_right
        other = even * from_right + (1 - even) * from_left
        return zs * 4 + first, (lat, z * 4 + other)

    def wd_take(zs, up):
        b = zs * 4 + x
        arrived(WD.at[b], wzr.at[zs])
        (wd_up if up else wd_down)(zs, b)
        wd_spread(zs, b)

    def wd_relay(zs):
        first, dev = relay_of(zs)
        arrived(WD.at[first], wxr.at[zs])
        send(WD.at[first], WD.at[first], wxs, wxr.at[8], dev)

    def take(zs, up):
        b = zs * 4 + x
        for k in range(3):
            rows = pl.ds(16 * k, 16)
            arrived(WU.at[b, rows], zr.at[zs, k])
            (pass_up if up else pass_down)(zs, b, rows, k)

    def relay(zs):
        first, dev = relay_of(zs)
        arrived(WU.at[first], xr.at[zs])
        send(WU.at[first], WU.at[first], xs, xr.at[8 + zs], dev)

    def rest(zs):
        arrived(WU.at[pl.ds(0, 2)], xr.at[8 + zs])

    c_own = pl.ds(pl.multiple_of(c * 128, 128), 128)
    c_other = pl.ds(pl.multiple_of((1 - c) * 128, 128), 128)

    def y_rows(yt):
        return pl.ds(pl.multiple_of(yt * 32, 32), 32)

    def sum0(j, value):
        DP[j] = value.astype(BF16)
        send(DP.at[j, c_other], RC.at[j], cs, cr.at[j], cdev)

    def sum1(j):
        arrived(RC.at[j], cr.at[j])
        S1[j] = (DP[j, c_own].astype(F32) + RC[j].astype(F32)).astype(BF16)
        for d in (2, 1, 3):
            send(S1.at[j, y_rows((y + d) % 4)], RY.at[j, d - 1], ys, yr.at[j], ydev(d))

    def sum2(j):
        total = S1[j, y_rows(y)].astype(F32)
        arrived(RY.at[j], yr.at[j])
        for d in range(3):
            total = total + RY[j, d].astype(F32)
        S2[j] = total.astype(BF16)
        send(S2.at[j], RZ.at[j], hs, hr.at[j], hdev)

    def sum3(j):
        arrived(RZ.at[j], hr.at[j])
        RES[j] = S2[j].astype(F32) + RZ[j].astype(F32)

    def each(f):
        lax.fori_loop(0, 4, lambda q, v: (f(q), v)[1], 0)

    def down(q):
        w = WD[pl.ds(8 * q, 8)].reshape(CH, FEAT)
        sum0(q, lax.dot_general(hid[...], w, NT, preferred_element_type=F32))

    def up_back(q):
        w = WU[pl.ds(8 * q, 8)].reshape(CH, COLS)
        sum0(4 + q, lax.dot_general(cot[...], w, NT, preferred_element_type=F32))

    def tok(yt):
        return pl.ds(pl.multiple_of(c * 128 + yt * 32, 32), 32)

    mine = tok(y)

    def gather1(m, part):
        for d in (2, 1, 3):
            send(part(mine), part(mine), ays, ayr.at[m], ydev(d))

    def gather2(m, part):
        arrived(part(pl.ds(0, 96)), ayr.at[m])
        send(part(c_own), part(c_own), acs, acr.at[m], cdev)

    def gather3(m, part):
        arrived(part(c_other), acr.at[m])

    def fwd(rows):
        return AGN.at[rows]

    def bwd(q):
        return lambda rows: AGE.at[q, rows]

    def norm():
        squares = jnp.zeros((32, 1), F32)
        for q in range(4):
            v = RES[q]
            squares = squares + jnp.sum(v * v, axis=1, keepdims=True)
        scales = lax.rsqrt(squares / R + 1e-06)
        SC[...] = jnp.broadcast_to(scales, (32, 128))
        for q in range(4):
            cols = slice(q * CH, (q + 1) * CH)
            AGN[mine, cols] = (RES[q] * scales * gain[:, cols]).astype(BF16)

    def q_cols(q):
        return pl.ds(pl.multiple_of(q * CH, CH), CH)

    def back3(q):
        sum3(4 + q)
        dn = RES[4 + q]
        scales = SC[:, 0:1]
        AGE[q, mine] = (scales * (gain[:, q_cols(q)] * dn)).astype(BF16)
        gather1(1 + q, bwd(q))
        GS[0, :, q_cols(q)] = jnp.sum(dn * RES[q] * scales, axis=0, keepdims=True)

    def back5(q):
        gather3(1 + q, bwd(q))
        n = AGN[:, q_cols(q)].astype(F32) * IG[:, q_cols(q)]
        part = jnp.sum(AGE[q].astype(F32) * n, axis=1, keepdims=True)
        INN[...] = INN[...] + jnp.broadcast_to(part, (TOK, 128))

    near_z = jnp.minimum(z, 7 - z)
    sign = jnp.where(z < 4, 1, -1)

    def in_turn(n, f):
        two = z + jnp.where(n % 2 == 1, -1, 1) * ((n + 1) // 2)
        one = z + sign * (n - near_z)

        @pl.when((n >= 0) & (n <= 7))
        def _():
            f(jnp.clip(jnp.where(n <= 2 * near_z, two, one), 0, 7))

    def turn(zs):
        d = jnp.abs(zs - z)
        return jnp.where(d > near_z, d + near_z, 2 * d - jnp.where(zs < z, 1, 0))

    def ready(q):
        return jnp.maximum(turn(2 * q), turn(2 * q + 1))

    def queries(n):
        cols = slice(n * CH, (n + 1) * CH)
        w = WU[:, :, cols].reshape(R, CH)
        qv[:, cols] = jnp.dot(AGN[...], w, preferred_element_type=F32).astype(BF16)

    q_copy = pltpu.make_async_copy(qv, q_out, loc.at[5])

    def weights_left():
        left(WU.at[pl.ds(0, 24)], xs)
        left(WD.at[pl.ds(0, 24)], wxs)

        @pl.when(near_z > 0)
        def _():
            left(WU.at[pl.ds(0, 9)], zs_sem)
            left(WD.at[pl.ds(0, 9)], wzs)

        @pl.when(near_z == 0)
        def _():
            left(WU.at[0], zs_sem)
            left(WD.at[0], wzs)

    def done_at(q):
        n = ready(q)
        return 4 + n - jnp.where(n >= 5, 1, 0) - jnp.where(n == 7, 1, 0)

    def run_at(i, when, f, *args):
        @pl.when(i == when)
        def _():
            f(*args)

    def chunks(i, lag, earliest, f):
        def chunk(q, v):
            run_at(i, jnp.maximum(done_at(q) + lag, earliest), f, q)
            return v

        lax.fori_loop(0, 4, chunk, 0)

    def step(i, carry):
        def at(when, f, *args):
            run_at(i, when, f, *args)

        def turns(table, f):
            for when, n in table:
                at(when, in_turn, jnp.int32(n), f)

        turns(((1, 1), (2, 2), (3, 3), (4, 4)), own_spread)
        for when, d in ((0, 2), (1, 3), (2, 4), (3, 5), (3, 6), (4, 7)):
            at(when, both, d, wd_take)
        both(i + 1, take)
        turns(((4, 5),), own_spread)
        turns(((0, 1), (1, 2), (2, 3), (3, 4), (4, 5), (4, 6), (5, 7)), wd_relay)
        turns(((5, 6), (6, 7)), own_spread)
        turns(((2, 0), (3, 1), (4, 2), (5, 3), (6, 4), (6, 5)), relay)
        at(7, second)
        turns(((7, 6), (7, 7)), relay)
        turns(((4, 0), (5, 1), (6, 2), (7, 3), (8, 4), (8, 5)), rest)
        at(8, third)
        turns(((9, 6), (9, 7)), rest)
        at(6, first)
        chunks(i, 0, 0, up_back)
        chunks(i, 1, 0, lambda q: sum1(4 + q))
        chunks(i, 2, 0, lambda q: sum2(4 + q))
        return carry

    def first():
        arrived(WD.at[pl.ds(0, 16)], wxr.at[8])
        each(down)

    def second():
        each(sum1)

    def third():
        each(sum2)

    def fourth():
        each(sum3)
        norm()
        gather1(0, fwd)

    def fifth():
        gather2(0, fwd)

    def sixth():
        gather3(0, fwd)

    both(1, wd_take)
    in_turn(0, wd_relay)
    lax.fori_loop(0, 10, step, 0)

    chunks(10, 1, 0, lambda q: sum1(4 + q))
    chunks(10, 2, 0, lambda q: sum2(4 + q))
    weights_left()
    chunks(11, 2, 0, lambda q: sum2(4 + q))
    fourth()
    chunks(11, 3, 11, back3)
    chunks(12, 3, 11, back3)
    for n, dev in enumerate(group):
        send(GS.at[0], GR.at[n], gs, gr, dev)
    fifth()
    chunks(12, 4, 12, lambda q: gather2(1 + q, bwd(q)))
    sixth()
    queries(0)
    queries(1)
    chunks(13, 4, 12, lambda q: gather2(1 + q, bwd(q)))
    total = GS[0]
    arrived(GR, gr)
    for n in range(31):
        total = total + GR[n]
    GS[1] = total
    for k in range(16):
        @pl.when(lat == k)
        def _():
            GZ[0] = GS[1, :, k * SHARE:(k + 1) * SHARE]

    for d in range(1, 8):
        send(GZ.at[0], GZ.at[d], gzs, gzr, zdev((z + d) % 8))
    chunks(13, 5, 13, back5)
    chunks(14, 5, 13, back5)
    inner = INN[:, 0:1] / R
    for q in range(4):
        cols = slice(q * CH, (q + 1) * CH)
        n = AGN[:, cols].astype(F32) * IG[:, cols]
        DL[:, cols] = (AGE[q].astype(F32) - n * inner).astype(BF16)
    dh = jnp.dot(DL[...], WD[...].reshape(R, FEAT), preferred_element_type=F32).astype(BF16)
    dhv[...] = lax.dot_general(unit(FEAT), dh, NT, preferred_element_type=F32).astype(BF16)
    dh_copy = pltpu.make_async_copy(dhv, dh_out, loc.at[0])
    dh_copy.start()
    queries(2)
    queries(3)
    q_copy.start()
    left(RC, cs)
    left(RY, ys)
    left(RZ, hs)
    left(AGN.at[pl.ds(0, 192)], ays)
    left(AGN, acs)
    left(GR, gs)
    left(GZ.at[pl.ds(0, 7)], gzs)
    arrived(GZ.at[pl.ds(1, 7)], gzr)
    share = GZ[0]
    for d in range(1, 8):
        share = share + GZ[d]
    dg_out[...] = share
    q_copy.wait()
    dh_copy.wait()


def body(hidden, w_down, w_up, norm_gain, cotangent):
    vmem = pl.BlockSpec(memory_space=pltpu.VMEM)
    hbm = pl.BlockSpec(memory_space=pltpu.HBM)
    dma = pltpu.SemaphoreType.DMA
    queries, dhidden, dgain = pl.pallas_call(
        kernel,
        name="query_path",
        out_shape=(
            jax.ShapeDtypeStruct((TOK, COLS), BF16),
            jax.ShapeDtypeStruct((FEAT, TOK), BF16),
            jax.ShapeDtypeStruct((1, SHARE), F32),
        ),
        in_specs=[hbm] * 5,
        out_specs=(hbm, hbm, vmem),
        scratch_shapes=[
            pltpu.VMEM((TOK, FEAT), BF16),
            pltpu.VMEM((FEAT, TOK), BF16),
            pltpu.VMEM((R,), F32),
            pltpu.VMEM((1, R), F32),
            pltpu.VMEM((TOK, COLS), BF16),
            pltpu.VMEM((TOK, COLS), BF16),
            pltpu.VMEM((FEAT, TOK), BF16),
            pltpu.VMEM((32, ROWS, COLS), BF16),
            pltpu.VMEM((32, ROWS, FEAT), BF16),
            pltpu.VMEM((8, TOK, CH), BF16),
            pltpu.VMEM((8, 128, CH), BF16),
            pltpu.VMEM((8, 128, CH), BF16),
            pltpu.VMEM((8, 3, 32, CH), BF16),
            pltpu.VMEM((8, 32, CH), BF16),
            pltpu.VMEM((8, 32, CH), BF16),
            pltpu.VMEM((8, 32, CH), F32),
            pltpu.VMEM((TOK, R), BF16),
            pltpu.VMEM((4, TOK, CH), BF16),
            pltpu.VMEM((TOK, R), BF16),
            pltpu.VMEM((32, 128), F32),
            pltpu.VMEM((1, R), F32),
            pltpu.VMEM((TOK, 128), F32),
            pltpu.VMEM((2, 1, R), F32),
            pltpu.VMEM((31, 1, R), F32),
            pltpu.VMEM((8, 1, SHARE), F32),
            dma((6,)), dma((8, 3)), dma, dma((16,)), dma, dma((8,)), dma, dma((9,)), dma,
            dma, dma((8,)), dma, dma((8,)), dma, dma((8,)),
            dma, dma((5,)), dma, dma((5,)), dma, dma, dma, dma,
        ],
        compiler_params=pltpu.CompilerParams(
            collective_id=0, has_side_effects=True, vmem_limit_bytes=62 * 2**20
        ),
    )(hidden.T, w_down.T, w_up, norm_gain, cotangent)
    return queries, dhidden.T, dgain.reshape(SHARE)


def solution(mesh):
    placed = (P("head", "lat"), P("lat", "head"), P("head", "lat"), P(), P("head", "lat"))
    return jax.shard_map(
        body,
        mesh=mesh,
        in_specs=placed,
        out_specs=(P("head", "lat"), P("head", "lat"), P("lat")),
        check_vma=False,
    )
```

```python
import jax
import jax.numpy as jnp
from jax import lax
from jax.experimental import pallas as pl
from jax.experimental.pallas import tpu as pltpu
from jax.sharding import PartitionSpec as P

MESH = pl.DeviceIdType.MESH
R = 1536
ROWS = 48
TOK = 256
FEAT = 320
COLS = 1536
CH = 384
SHARE = 96
F32 = jnp.float32
BF16 = jnp.bfloat16
NT = (((1,), (1,)), ((), ()))


def unit(n):
    rows, cols = (lax.broadcasted_iota(jnp.int32, (n, n), d) for d in (0, 1))
    return (rows == cols).astype(BF16)


def kernel(
    hid_in, wd_in, wu_in, gain_in, cot_in,
    q_out, dh_out, dg_out,
    hid, hid_v, gain_v, gain, cot, qv, dhv,
    WU, WD, DP, RC, S1, RY, S2, RZ, RES, AGN, AGE, DL, SC, IG, INN, GS, GP, GR, GZ,
    loc, zr, zs_sem, xr, xs, wzr, wzs, wxr, wxs,
    cs, cr, ys, yr, hs, hr,
    ays, ayr, acs, acr, gs, gr, gzs, gzr,
):
    lat = lax.axis_index("lat")
    head = lax.axis_index("head")
    x, z = head % 4, head // 4
    y, zh, c = lat // 4, (lat // 2) % 2, lat % 2

    def xdev(d):
        return (lat, z * 4 + (x + d) % 4)

    def zdev(zt):
        return (lat, zt * 4 + x)

    def ydev(d):
        return (((y + d) % 4) * 4 + zh * 2 + c, head)

    cdev = (y * 4 + zh * 2 + (1 - c), head)
    hdev = (y * 4 + (1 - zh) * 2 + c, head)
    group = []
    for dx in range(4):
        for dy in range(4):
            for dc in range(2):
                core = c + dc * (1 - 2 * c)
                group.append((((y + dy) % 4) * 4 + zh * 2 + core, z * 4 + (x + dx) % 4))
    group = group[1:]

    def copy(src, dst, ss, rs, dev):
        return pltpu.make_async_remote_copy(
            src_ref=src, dst_ref=dst, send_sem=ss, recv_sem=rs, device_id=dev, device_id_type=MESH
        )

    def send(src, dst, ss, rs, dev):
        copy(src, dst, ss, rs, dev).start()

    def arrived(dst, rs):
        copy(dst, dst, rs, rs, cdev).wait_recv()

    def left(src, ss):
        copy(src, src, ss, ss, cdev).wait_send()

    bar = pltpu.get_barrier_semaphore()
    partners = group + [hdev]
    partners += [zdev((z + d) % 8) for d in range(1, 8)]
    for dev in partners:
        pl.semaphore_signal(bar, inc=1, device_id=dev, device_id_type=MESH)
    me = head
    inputs = [
        pltpu.make_async_copy(src, dst, loc.at[n])
        for n, (src, dst) in enumerate(
            ((wd_in, WD.at[me]), (wu_in, WU.at[me]), (hid_in, hid_v), (gain_in, gain_v), (cot_in, cot))
        )
    ]
    for cp in inputs:
        cp.start()
    for cp in inputs:
        cp.wait()
    hid[...] = lax.dot_general(unit(TOK), hid_v[...], NT, preferred_element_type=F32).astype(BF16)
    gain[...] = gain_v[...].reshape(1, R)
    IG[...] = 1.0 / gain[...]
    INN[...] = jnp.zeros_like(INN)
    pl.semaphore_wait(bar, len(partners))

    def pass_up(zs, b, rows, k):
        @pl.when(z < 7)
        def _():
            send(WU.at[b, rows], WU.at[b, rows], zs_sem, zr.at[zs, k], zdev(jnp.minimum(z + 1, 7)))

    def pass_down(zs, b, rows, k):
        @pl.when(z > 0)
        def _():
            send(WU.at[b, rows], WU.at[b, rows], zs_sem, zr.at[zs, k], zdev(jnp.maximum(z - 1, 0)))

    def wd_up(zs, b):
        @pl.when(z < 7)
        def _():
            send(WD.at[b], WD.at[b], wzs, wzr.at[zs], zdev(jnp.minimum(z + 1, 7)))

    def wd_down(zs, b):
        @pl.when(z > 0)
        def _():
            send(WD.at[b], WD.at[b], wzs, wzr.at[zs], zdev(jnp.maximum(z - 1, 0)))

    wd_up(z, me)
    wd_down(z, me)
    for k in range(3):
        pass_up(z, me, pl.ds(16 * k, 16), k)
        pass_down(z, me, pl.ds(16 * k, 16), k)

    def spread(zs, b):
        even = 1 - zs % 2
        send(WU.at[b], WU.at[b], xs, xr.at[zs + 8 * (1 - even)], xdev(1))
        send(WU.at[b], WU.at[b], xs, xr.at[zs + 8 * even], xdev(3))

    def own_spread(zs):
        spread(zs, zs * 4 + x)

    def wd_spread(zs, b):
        even = 1 - zs % 2
        send(WD.at[b], WD.at[b], wxs, wxr.at[even * zs + 8 * (1 - even)], xdev(1))
        send(WD.at[b], WD.at[b], wxs, wxr.at[(1 - even) * zs + 8 * even], xdev(3))

    wd_spread(z, me)
    spread(z, me)

    def both(s, f):
        lo, hi = z - s, z + s

        @pl.when((s >= 0) & (lo >= 0))
        def _():
            f(jnp.clip(lo, 0, 7), True)

        @pl.when((s >= 1) & (hi <= 7))
        def _():
            f(jnp.clip(hi, 0, 7), False)

    def relay_of(zs):
        even = 1 - zs % 2
        from_left, from_right = (x + 3) % 4, (x + 1) % 4
        first = even * from_left + (1 - even) * from_right
        other = even * from_right + (1 - even) * from_left
        return zs * 4 + first, (lat, z * 4 + other)

    def wd_take(zs, up):
        b = zs * 4 + x
        arrived(WD.at[b], wzr.at[zs])
        (wd_up if up else wd_down)(zs, b)
        wd_spread(zs, b)

    def wd_relay(zs):
        first, dev = relay_of(zs)
        arrived(WD.at[first], wxr.at[zs])
        send(WD.at[first], WD.at[first], wxs, wxr.at[8], dev)

    def take(zs, up):
        b = zs * 4 + x
        for k in range(3):
            rows = pl.ds(16 * k, 16)
            arrived(WU.at[b, rows], zr.at[zs, k])
            (pass_up if up else pass_down)(zs, b, rows, k)

    def relay(zs):
        first, dev = relay_of(zs)
        arrived(WU.at[first], xr.at[zs])
        send(WU.at[first], WU.at[first], xs, xr.at[8 + zs], dev)

    def rest(zs):
        arrived(WU.at[pl.ds(0, 2)], xr.at[8 + zs])

    c_own = pl.ds(pl.multiple_of(c * 128, 128), 128)
    c_other = pl.ds(pl.multiple_of((1 - c) * 128, 128), 128)

    def y_rows(yt):
        return pl.ds(pl.multiple_of(yt * 32, 32), 32)

    def sum0(j, value):
        DP[j] = value.astype(BF16)
        send(DP.at[j, c_other], RC.at[j], cs, cr.at[j], cdev)

    def sum1(j):
        arrived(RC.at[j], cr.at[j])
        S1[j] = (DP[j, c_own].astype(F32) + RC[j].astype(F32)).astype(BF16)
        for d in (2, 1, 3):
            send(S1.at[j, y_rows((y + d) % 4)], RY.at[j, d - 1], ys, yr.at[j], ydev(d))

    def sum2(j):
        total = S1[j, y_rows(y)].astype(F32)
        arrived(RY.at[j], yr.at[j])
        for d in range(3):
            total = total + RY[j, d].astype(F32)
        S2[j] = total.astype(BF16)
        send(S2.at[j], RZ.at[j], hs, hr.at[j], hdev)

    def sum3(j):
        arrived(RZ.at[j], hr.at[j])
        RES[j] = S2[j].astype(F32) + RZ[j].astype(F32)

    def each(f):
        lax.fori_loop(0, 4, lambda q, v: (f(q), v)[1], 0)

    def down(q):
        w = WD[pl.ds(8 * q, 8)].reshape(CH, FEAT)
        sum0(q, lax.dot_general(hid[...], w, NT, preferred_element_type=F32))

    def up_back(q):
        w = WU[pl.ds(8 * q, 8)].reshape(CH, COLS)
        sum0(4 + q, lax.dot_general(cot[...], w, NT, preferred_element_type=F32))

    def tok(yt):
        return pl.ds(pl.multiple_of(c * 128 + yt * 32, 32), 32)

    mine = tok(y)

    def gather1(m, part):
        for d in (2, 1, 3):
            send(part(mine), part(mine), ays, ayr.at[m], ydev(d))

    def gather2(m, part):
        arrived(part(pl.ds(0, 96)), ayr.at[m])
        send(part(c_own), part(c_own), acs, acr.at[m], cdev)

    def gather3(m, part):
        arrived(part(c_other), acr.at[m])

    def fwd(rows):
        return AGN.at[rows]

    def bwd(q):
        return lambda rows: AGE.at[q, rows]

    def norm():
        squares = jnp.zeros((32, 1), F32)
        for q in range(4):
            v = RES[q]
            squares = squares + jnp.sum(v * v, axis=1, keepdims=True)
        scales = lax.rsqrt(squares / R + 1e-06)
        SC[...] = jnp.broadcast_to(scales, (32, 128))
        for q in range(4):
            cols = slice(q * CH, (q + 1) * CH)
            AGN[mine, cols] = (RES[q] * scales * gain[:, cols]).astype(BF16)

    def q_cols(q):
        return pl.ds(pl.multiple_of(q * CH, CH), CH)

    def back3(q):
        sum3(4 + q)
        dn = RES[4 + q]
        scales = SC[:, 0:1]
        AGE[q, mine] = (scales * (gain[:, q_cols(q)] * dn)).astype(BF16)
        gather1(1 + q, bwd(q))
        GS[:, q_cols(q)] = jnp.sum(dn * RES[q] * scales, axis=0, keepdims=True)

    def back5(q):
        gather3(1 + q, bwd(q))
        n = AGN[:, q_cols(q)].astype(F32) * IG[:, q_cols(q)]
        part = jnp.sum(AGE[q].astype(F32) * n, axis=1, keepdims=True)
        INN[...] = INN[...] + jnp.broadcast_to(part, (TOK, 128))

    near_z = jnp.minimum(z, 7 - z)
    sign = jnp.where(z < 4, 1, -1)

    def in_turn(n, f):
        two = z + jnp.where(n % 2 == 1, -1, 1) * ((n + 1) // 2)
        one = z + sign * (n - near_z)

        @pl.when((n >= 0) & (n <= 7))
        def _():
            f(jnp.clip(jnp.where(n <= 2 * near_z, two, one), 0, 7))

    def turn(zs):
        d = jnp.abs(zs - z)
        return jnp.where(d > near_z, d + near_z, 2 * d - jnp.where(zs < z, 1, 0))

    def ready(q):
        return jnp.maximum(turn(2 * q), turn(2 * q + 1))

    def queries(n):
        cols = slice(n * CH, (n + 1) * CH)
        w = WU[:, :, cols].reshape(R, CH)
        qv[:, cols] = jnp.dot(AGN[...], w, preferred_element_type=F32).astype(BF16)

    q_copy = pltpu.make_async_copy(qv, q_out, loc.at[5])

    def weights_left():
        left(WU.at[pl.ds(0, 24)], xs)
        left(WD.at[pl.ds(0, 24)], wxs)

        @pl.when(near_z > 0)
        def _():
            left(WU.at[pl.ds(0, 9)], zs_sem)
            left(WD.at[pl.ds(0, 9)], wzs)

        @pl.when(near_z == 0)
        def _():
            left(WU.at[0], zs_sem)
            left(WD.at[0], wzs)

    def done_at(q):
        n = ready(q)
        return 4 + n - jnp.where(n >= 5, 1, 0) - jnp.where(n == 7, 1, 0)

    def run_at(i, when, f, *args):
        @pl.when(i == when)
        def _():
            f(*args)

    def chunks(i, lag, earliest, f):
        def chunk(q, v):
            run_at(i, jnp.maximum(done_at(q) + lag, earliest), f, q)
            return v

        lax.fori_loop(0, 4, chunk, 0)

    def step(i, carry):
        def at(when, f, *args):
            run_at(i, when, f, *args)

        def turns(table, f):
            for when, n in table:
                at(when, in_turn, jnp.int32(n), f)

        turns(((1, 1), (2, 2), (3, 3), (4, 4)), own_spread)
        for when, d in ((0, 2), (1, 3), (2, 4), (3, 5), (3, 6), (4, 7)):
            at(when, both, d, wd_take)
        both(i + 1, take)
        turns(((4, 5),), own_spread)
        turns(((0, 1), (1, 2), (2, 3), (3, 4), (4, 5), (4, 6), (5, 7)), wd_relay)
        turns(((5, 6), (6, 7)), own_spread)
        turns(((2, 0), (3, 1), (4, 2), (5, 3), (6, 4), (6, 5)), relay)
        at(7, second)
        turns(((7, 6), (7, 7)), relay)
        turns(((4, 0), (5, 1), (6, 2), (7, 3), (8, 4), (8, 5)), rest)
        at(8, third)
        turns(((9, 6), (9, 7)), rest)
        at(6, first)
        chunks(i, 0, 0, up_back)
        chunks(i, 1, 0, lambda q: sum1(4 + q))
        chunks(i, 2, 0, lambda q: sum2(4 + q))
        return carry

    def first():
        arrived(WD.at[pl.ds(0, 16)], wxr.at[8])
        each(down)

    def second():
        each(sum1)

    def third():
        each(sum2)

    def fourth():
        each(sum3)
        norm()
        gather1(0, fwd)

    def fifth():
        gather2(0, fwd)

    def sixth():
        gather3(0, fwd)

    both(1, wd_take)
    in_turn(0, wd_relay)
    lax.fori_loop(0, 10, step, 0)

    chunks(10, 1, 0, lambda q: sum1(4 + q))
    chunks(10, 2, 0, lambda q: sum2(4 + q))
    weights_left()
    chunks(11, 2, 0, lambda q: sum2(4 + q))
    fourth()
    chunks(11, 3, 11, back3)
    chunks(12, 3, 11, back3)
    for k in range(16):
        GP[k] = GS[:, k * SHARE:(k + 1) * SHARE]
    for n, dev in enumerate(group):
        send(GP.at[dev[0]], GR.at[n], gs, gr, dev)
    fifth()
    chunks(12, 4, 12, lambda q: gather2(1 + q, bwd(q)))
    sixth()
    queries(0)
    queries(1)
    chunks(13, 4, 12, lambda q: gather2(1 + q, bwd(q)))
    arrived(GR, gr)
    share = GP[lat]
    for n in range(31):
        share = share + GR[n]
    GZ[0] = share
    for d in range(1, 8):
        send(GZ.at[0], GZ.at[d], gzs, gzr, zdev((z + d) % 8))
    chunks(13, 5, 13, back5)
    chunks(14, 5, 13, back5)
    inner = INN[:, 0:1] / R
    for q in range(4):
        cols = slice(q * CH, (q + 1) * CH)
        n = AGN[:, cols].astype(F32) * IG[:, cols]
        DL[:, cols] = (AGE[q].astype(F32) - n * inner).astype(BF16)
    dh = jnp.dot(DL[...], WD[...].reshape(R, FEAT), preferred_element_type=F32).astype(BF16)
    dhv[...] = lax.dot_general(unit(FEAT), dh, NT, preferred_element_type=F32).astype(BF16)
    dh_copy = pltpu.make_async_copy(dhv, dh_out, loc.at[0])
    dh_copy.start()
    queries(2)
    queries(3)
    q_copy.start()
    left(RC, cs)
    left(RY, ys)
    left(RZ, hs)
    left(AGN.at[pl.ds(0, 192)], ays)
    left(AGN, acs)
    left(GR, gs)
    left(GZ.at[pl.ds(0, 7)], gzs)
    arrived(GZ.at[pl.ds(1, 7)], gzr)
    share = GZ[0]
    for d in range(1, 8):
        share = share + GZ[d]
    dg_out[...] = share
    q_copy.wait()
    dh_copy.wait()


def body(hidden, w_down, w_up, norm_gain, cotangent):
    vmem = pl.BlockSpec(memory_space=pltpu.VMEM)
    hbm = pl.BlockSpec(memory_space=pltpu.HBM)
    dma = pltpu.SemaphoreType.DMA
    queries, dhidden, dgain = pl.pallas_call(
        kernel,
        name="query_path",
        out_shape=(
            jax.ShapeDtypeStruct((TOK, COLS), BF16),
            jax.ShapeDtypeStruct((FEAT, TOK), BF16),
            jax.ShapeDtypeStruct((1, SHARE), F32),
        ),
        in_specs=[hbm] * 5,
        out_specs=(hbm, hbm, vmem),
        scratch_shapes=[
            pltpu.VMEM((TOK, FEAT), BF16),
            pltpu.VMEM((FEAT, TOK), BF16),
            pltpu.VMEM((R,), F32),
            pltpu.VMEM((1, R), F32),
            pltpu.VMEM((TOK, COLS), BF16),
            pltpu.VMEM((TOK, COLS), BF16),
            pltpu.VMEM((FEAT, TOK), BF16),
            pltpu.VMEM((32, ROWS, COLS), BF16),
            pltpu.VMEM((32, ROWS, FEAT), BF16),
            pltpu.VMEM((8, TOK, CH), BF16),
            pltpu.VMEM((8, 128, CH), BF16),
            pltpu.VMEM((8, 128, CH), BF16),
            pltpu.VMEM((8, 3, 32, CH), BF16),
            pltpu.VMEM((8, 32, CH), BF16),
            pltpu.VMEM((8, 32, CH), BF16),
            pltpu.VMEM((8, 32, CH), F32),
            pltpu.VMEM((TOK, R), BF16),
            pltpu.VMEM((4, TOK, CH), BF16),
            pltpu.VMEM((TOK, R), BF16),
            pltpu.VMEM((32, 128), F32),
            pltpu.VMEM((1, R), F32),
            pltpu.VMEM((TOK, 128), F32),
            pltpu.VMEM((1, R), F32),
            pltpu.VMEM((16, 1, SHARE), F32),
            pltpu.VMEM((31, 1, SHARE), F32),
            pltpu.VMEM((8, 1, SHARE), F32),
            dma((6,)), dma((8, 3)), dma, dma((16,)), dma, dma((8,)), dma, dma((9,)), dma,
            dma, dma((8,)), dma, dma((8,)), dma, dma((8,)),
            dma, dma((5,)), dma, dma((5,)), dma, dma, dma, dma,
        ],
        compiler_params=pltpu.CompilerParams(
            collective_id=0, has_side_effects=True, vmem_limit_bytes=62 * 2**20
        ),
    )(hidden.T, w_down.T, w_up, norm_gain, cotangent)
    return queries, dhidden.T, dgain.reshape(SHARE)


def solution(mesh):
    placed = (P("head", "lat"), P("lat", "head"), P("head", "lat"), P(), P("head", "lat"))
    return jax.shard_map(
        body,
        mesh=mesh,
        in_specs=placed,
        out_specs=(P("head", "lat"), P("head", "lat"), P("lat")),
        check_vma=False,
    )
```

```python
import jax
import jax.numpy as jnp
from jax import lax
from jax.experimental import pallas as pl
from jax.experimental.pallas import tpu as pltpu
from jax.sharding import PartitionSpec as P

MESH = pl.DeviceIdType.MESH
R = 1536
ROWS = 48
TOK = 256
FEAT = 320
COLS = 1536
CH = 384
SHARE = 96
F32 = jnp.float32
BF16 = jnp.bfloat16
NT = (((1,), (1,)), ((), ()))


def unit(n):
    rows, cols = (lax.broadcasted_iota(jnp.int32, (n, n), d) for d in (0, 1))
    return (rows == cols).astype(BF16)


def kernel(
    hid_in, wd_in, wu_in, gain_in, cot_in,
    q_out, dh_out, dg_out,
    hid, hid_v, gain_v, gain, cot, qv, dhv,
    WU, WD, DP, RC, S1, RY, S2, RZ, RES, AGN, AGE, DL, SC, IG, INN, GS, GP, GR, GZ,
    loc, zr, zs_sem, xr, xs, wzr, wzs, wxr, wxs,
    cs, cr, ys, yr, hs, hr,
    ays, ayr, acs, acr, gs, gr, gzs, gzr,
):
    lat = lax.axis_index("lat")
    head = lax.axis_index("head")
    x, z = head % 4, head // 4
    y, zh, c = lat // 4, (lat // 2) % 2, lat % 2

    def xdev(d):
        return (lat, z * 4 + (x + d) % 4)

    def zdev(zt):
        return (lat, zt * 4 + x)

    def ydev(d):
        return (((y + d) % 4) * 4 + zh * 2 + c, head)

    cdev = (y * 4 + zh * 2 + (1 - c), head)
    hdev = (y * 4 + (1 - zh) * 2 + c, head)
    group = []
    for dx in range(4):
        for dy in range(4):
            for dc in range(2):
                core = c + dc * (1 - 2 * c)
                group.append((((y + dy) % 4) * 4 + zh * 2 + core, z * 4 + (x + dx) % 4))
    group = group[1:]

    def copy(src, dst, ss, rs, dev):
        return pltpu.make_async_remote_copy(
            src_ref=src, dst_ref=dst, send_sem=ss, recv_sem=rs, device_id=dev, device_id_type=MESH
        )

    def send(src, dst, ss, rs, dev):
        copy(src, dst, ss, rs, dev).start()

    def arrived(dst, rs):
        copy(dst, dst, rs, rs, cdev).wait_recv()

    def left(src, ss):
        copy(src, src, ss, ss, cdev).wait_send()

    bar = pltpu.get_barrier_semaphore()
    partners = group + [hdev]
    partners += [zdev((z + d) % 8) for d in range(1, 8)]
    for dev in partners:
        pl.semaphore_signal(bar, inc=1, device_id=dev, device_id_type=MESH)
    me = head
    inputs = [
        pltpu.make_async_copy(src, dst, loc.at[n])
        for n, (src, dst) in enumerate(
            ((wd_in, WD.at[me]), (wu_in, WU.at[me]), (hid_in, hid_v), (gain_in, gain_v), (cot_in, cot))
        )
    ]
    for cp in inputs:
        cp.start()
    for cp in inputs:
        cp.wait()
    hid[...] = lax.dot_general(unit(TOK), hid_v[...], NT, preferred_element_type=F32).astype(BF16)
    gain[...] = gain_v[...].reshape(1, R)
    IG[...] = 1.0 / gain[...]
    INN[...] = jnp.zeros_like(INN)
    pl.semaphore_wait(bar, len(partners))

    def pass_up(zs, b, rows, k):
        @pl.when(z < 7)
        def _():
            send(WU.at[b, rows], WU.at[b, rows], zs_sem, zr.at[zs, k], zdev(jnp.minimum(z + 1, 7)))

    def pass_down(zs, b, rows, k):
        @pl.when(z > 0)
        def _():
            send(WU.at[b, rows], WU.at[b, rows], zs_sem, zr.at[zs, k], zdev(jnp.maximum(z - 1, 0)))

    def wd_up(zs, b):
        @pl.when(z < 7)
        def _():
            send(WD.at[b], WD.at[b], wzs, wzr.at[zs], zdev(jnp.minimum(z + 1, 7)))

    def wd_down(zs, b):
        @pl.when(z > 0)
        def _():
            send(WD.at[b], WD.at[b], wzs, wzr.at[zs], zdev(jnp.maximum(z - 1, 0)))

    wd_up(z, me)
    wd_down(z, me)
    for k in range(3):
        pass_up(z, me, pl.ds(16 * k, 16), k)
        pass_down(z, me, pl.ds(16 * k, 16), k)

    def spread(zs, b):
        even = 1 - zs % 2
        send(WU.at[b], WU.at[b], xs, xr.at[zs + 8 * (1 - even)], xdev(1))
        send(WU.at[b], WU.at[b], xs, xr.at[zs + 8 * even], xdev(3))

    def own_spread(zs):
        spread(zs, zs * 4 + x)

    def wd_spread(zs, b):
        even = 1 - zs % 2
        send(WD.at[b], WD.at[b], wxs, wxr.at[even * zs + 8 * (1 - even)], xdev(1))
        send(WD.at[b], WD.at[b], wxs, wxr.at[(1 - even) * zs + 8 * even], xdev(3))

    wd_spread(z, me)
    spread(z, me)

    def both(s, f):
        lo, hi = z - s, z + s

        @pl.when((s >= 0) & (lo >= 0))
        def _():
            f(jnp.clip(lo, 0, 7), True)

        @pl.when((s >= 1) & (hi <= 7))
        def _():
            f(jnp.clip(hi, 0, 7), False)

    def relay_of(zs):
        even = 1 - zs % 2
        from_left, from_right = (x + 3) % 4, (x + 1) % 4
        first = even * from_left + (1 - even) * from_right
        other = even * from_right + (1 - even) * from_left
        return zs * 4 + first, (lat, z * 4 + other)

    def wd_take(zs, up):
        b = zs * 4 + x
        arrived(WD.at[b], wzr.at[zs])
        (wd_up if up else wd_down)(zs, b)
        wd_spread(zs, b)

    def wd_relay(zs):
        first, dev = relay_of(zs)
        arrived(WD.at[first], wxr.at[zs])
        send(WD.at[first], WD.at[first], wxs, wxr.at[8], dev)

    def take(zs, up):
        b = zs * 4 + x
        for k in range(3):
            rows = pl.ds(16 * k, 16)
            arrived(WU.at[b, rows], zr.at[zs, k])
            (pass_up if up else pass_down)(zs, b, rows, k)

    def relay(zs):
        first, dev = relay_of(zs)
        arrived(WU.at[first], xr.at[zs])
        send(WU.at[first], WU.at[first], xs, xr.at[8 + zs], dev)

    def rest(zs):
        arrived(WU.at[pl.ds(0, 2)], xr.at[8 + zs])

    c_own = pl.ds(pl.multiple_of(c * 128, 128), 128)
    c_other = pl.ds(pl.multiple_of((1 - c) * 128, 128), 128)

    def y_rows(yt):
        return pl.ds(pl.multiple_of(yt * 32, 32), 32)

    def sum0(j, value):
        DP[j] = value.astype(BF16)
        send(DP.at[j, c_other], RC.at[j], cs, cr.at[j], cdev)

    def sum1(j):
        arrived(RC.at[j], cr.at[j])
        S1[j] = (DP[j, c_own].astype(F32) + RC[j].astype(F32)).astype(BF16)
        for d in (2, 1, 3):
            send(S1.at[j, y_rows((y + d) % 4)], RY.at[j, d - 1], ys, yr.at[j], ydev(d))

    def sum2(j):
        total = S1[j, y_rows(y)].astype(F32)
        arrived(RY.at[j], yr.at[j])
        for d in range(3):
            total = total + RY[j, d].astype(F32)
        S2[j] = total.astype(BF16)
        send(S2.at[j], RZ.at[j], hs, hr.at[j], hdev)

    def sum3(j):
        arrived(RZ.at[j], hr.at[j])
        RES[j] = S2[j].astype(F32) + RZ[j].astype(F32)

    def each(f):
        lax.fori_loop(0, 4, lambda q, v: (f(q), v)[1], 0)

    def down(q):
        w = WD[pl.ds(8 * q, 8)].reshape(CH, FEAT)
        sum0(q, lax.dot_general(hid[...], w, NT, preferred_element_type=F32))

    def up_back(q):
        w = WU[pl.ds(8 * q, 8)].reshape(CH, COLS)
        sum0(4 + q, lax.dot_general(cot[...], w, NT, preferred_element_type=F32))

    def tok(yt):
        return pl.ds(pl.multiple_of(c * 128 + yt * 32, 32), 32)

    mine = tok(y)

    def gather1(m, part):
        for d in (2, 1, 3):
            send(part(mine), part(mine), ays, ayr.at[m], ydev(d))

    def gather2(m, part):
        arrived(part(pl.ds(0, 96)), ayr.at[m])
        send(part(c_own), part(c_own), acs, acr.at[m], cdev)

    def gather3(m, part):
        arrived(part(c_other), acr.at[m])

    def fwd(rows):
        return AGN.at[rows]

    def bwd(q):
        return lambda rows: AGE.at[q, rows]

    def norm():
        squares = jnp.zeros((32, 1), F32)
        for q in range(4):
            v = RES[q]
            squares = squares + jnp.sum(v * v, axis=1, keepdims=True)
        scales = lax.rsqrt(squares / R + 1e-06)
        SC[...] = jnp.broadcast_to(scales, (32, 128))
        for q in range(4):
            cols = slice(q * CH, (q + 1) * CH)
            AGN[mine, cols] = (RES[q] * scales * gain[:, cols]).astype(BF16)

    def q_cols(q):
        return pl.ds(pl.multiple_of(q * CH, CH), CH)

    def back3(q):
        sum3(4 + q)
        dn = RES[4 + q]
        scales = SC[:, 0:1]
        AGE[q, mine] = (scales * (gain[:, q_cols(q)] * dn)).astype(BF16)
        gather1(1 + q, bwd(q))
        GS[:, q_cols(q)] = jnp.sum(dn * RES[q] * scales, axis=0, keepdims=True)

    def back5(q):
        gather3(1 + q, bwd(q))
        n = AGN[:, q_cols(q)].astype(F32) * IG[:, q_cols(q)]
        part = jnp.sum(AGE[q].astype(F32) * n, axis=1, keepdims=True)
        INN[...] = INN[...] + jnp.broadcast_to(part, (TOK, 128))

    near_z = jnp.minimum(z, 7 - z)
    sign = jnp.where(z < 4, 1, -1)

    def in_turn(n, f):
        two = z + jnp.where(n % 2 == 1, -1, 1) * ((n + 1) // 2)
        one = z + sign * (n - near_z)

        @pl.when((n >= 0) & (n <= 7))
        def _():
            f(jnp.clip(jnp.where(n <= 2 * near_z, two, one), 0, 7))

    def turn(zs):
        d = jnp.abs(zs - z)
        return jnp.where(d > near_z, d + near_z, 2 * d - jnp.where(zs < z, 1, 0))

    def ready(q):
        return jnp.maximum(turn(2 * q), turn(2 * q + 1))

    def queries(n):
        cols = slice(n * CH, (n + 1) * CH)
        w = WU[:, :, cols].reshape(R, CH)
        qv[:, cols] = jnp.dot(AGN[...], w, preferred_element_type=F32).astype(BF16)

    q_copy = pltpu.make_async_copy(qv, q_out, loc.at[5])

    def weights_left():
        left(WU.at[pl.ds(0, 24)], xs)
        left(WD.at[pl.ds(0, 24)], wxs)

        @pl.when(near_z > 0)
        def _():
            left(WU.at[pl.ds(0, 9)], zs_sem)
            left(WD.at[pl.ds(0, 9)], wzs)

        @pl.when(near_z == 0)
        def _():
            left(WU.at[0], zs_sem)
            left(WD.at[0], wzs)

    def done_at(q):
        n = ready(q)
        return 4 + n - jnp.where(n >= 5, 1, 0) - jnp.where(n == 7, 1, 0)

    def run_at(i, when, f, *args):
        @pl.when(i == when)
        def _():
            f(*args)

    def chunks(i, lag, earliest, f):
        def chunk(q, v):
            run_at(i, jnp.maximum(done_at(q) + lag, earliest), f, q)
            return v

        lax.fori_loop(0, 4, chunk, 0)

    def step(i, carry):
        def at(when, f, *args):
            run_at(i, when, f, *args)

        def turns(table, f):
            for when, n in table:
                at(when, in_turn, jnp.int32(n), f)

        turns(((1, 1), (2, 2), (3, 3), (4, 4)), own_spread)
        for when, d in ((0, 2), (1, 3), (2, 4), (3, 5), (3, 6), (4, 7)):
            at(when, both, d, wd_take)
        both(i + 1, take)
        turns(((4, 5),), own_spread)
        turns(((0, 1), (1, 2), (2, 3), (3, 4), (4, 5), (4, 6), (5, 7)), wd_relay)
        turns(((5, 6), (6, 7)), own_spread)
        turns(((2, 0), (3, 1), (4, 2), (5, 3), (6, 4), (6, 5)), relay)
        at(7, second)
        turns(((7, 6), (7, 7)), relay)
        turns(((4, 0), (5, 1), (6, 2), (7, 3), (8, 4), (8, 5)), rest)
        at(8, third)
        turns(((9, 6), (9, 7)), rest)
        at(6, first)
        chunks(i, 0, 0, up_back)
        chunks(i, 1, 0, lambda q: sum1(4 + q))
        chunks(i, 2, 0, lambda q: sum2(4 + q))
        return carry

    def first():
        arrived(WD.at[pl.ds(0, 16)], wxr.at[8])
        each(down)

    def second():
        each(sum1)

    def third():
        each(sum2)

    def fourth():
        each(sum3)
        norm()
        gather1(0, fwd)

    def fifth():
        gather2(0, fwd)

    def sixth():
        gather3(0, fwd)

    both(1, wd_take)
    in_turn(0, wd_relay)
    lax.fori_loop(0, 10, step, 0)

    chunks(10, 1, 0, lambda q: sum1(4 + q))
    chunks(10, 2, 0, lambda q: sum2(4 + q))
    weights_left()
    chunks(11, 2, 0, lambda q: sum2(4 + q))
    fourth()
    chunks(11, 3, 11, back3)
    chunks(12, 3, 11, back3)
    for k in range(16):
        GP[k] = GS[:, k * SHARE:(k + 1) * SHARE]
    for n, dev in enumerate(group):
        send(GP.at[dev[0]], GR.at[n], gs, gr, dev)
    fifth()
    chunks(12, 4, 12, lambda q: gather2(1 + q, bwd(q)))
    chunks(13, 4, 12, lambda q: gather2(1 + q, bwd(q)))
    sixth()
    arrived(GR, gr)
    share = GP[lat]
    for n in range(31):
        share = share + GR[n]
    GZ[0] = share
    for d in range(1, 8):
        send(GZ.at[0], GZ.at[d], gzs, gzr, zdev((z + d) % 8))
    queries(0)
    queries(1)
    chunks(13, 5, 13, back5)
    chunks(14, 5, 13, back5)
    inner = INN[:, 0:1] / R
    for q in range(4):
        cols = slice(q * CH, (q + 1) * CH)
        n = AGN[:, cols].astype(F32) * IG[:, cols]
        DL[:, cols] = (AGE[q].astype(F32) - n * inner).astype(BF16)
    dh = jnp.dot(DL[...], WD[...].reshape(R, FEAT), preferred_element_type=F32).astype(BF16)
    dhv[...] = lax.dot_general(unit(FEAT), dh, NT, preferred_element_type=F32).astype(BF16)
    dh_copy = pltpu.make_async_copy(dhv, dh_out, loc.at[0])
    dh_copy.start()
    queries(2)
    queries(3)
    q_copy.start()
    left(RC, cs)
    left(RY, ys)
    left(RZ, hs)
    left(AGN.at[pl.ds(0, 192)], ays)
    left(AGN, acs)
    left(GR, gs)
    left(GZ.at[pl.ds(0, 7)], gzs)
    arrived(GZ.at[pl.ds(1, 7)], gzr)
    share = GZ[0]
    for d in range(1, 8):
        share = share + GZ[d]
    dg_out[...] = share
    q_copy.wait()
    dh_copy.wait()


def body(hidden, w_down, w_up, norm_gain, cotangent):
    vmem = pl.BlockSpec(memory_space=pltpu.VMEM)
    hbm = pl.BlockSpec(memory_space=pltpu.HBM)
    dma = pltpu.SemaphoreType.DMA
    queries, dhidden, dgain = pl.pallas_call(
        kernel,
        name="query_path",
        out_shape=(
            jax.ShapeDtypeStruct((TOK, COLS), BF16),
            jax.ShapeDtypeStruct((FEAT, TOK), BF16),
            jax.ShapeDtypeStruct((1, SHARE), F32),
        ),
        in_specs=[hbm] * 5,
        out_specs=(hbm, hbm, vmem),
        scratch_shapes=[
            pltpu.VMEM((TOK, FEAT), BF16),
            pltpu.VMEM((FEAT, TOK), BF16),
            pltpu.VMEM((R,), F32),
            pltpu.VMEM((1, R), F32),
            pltpu.VMEM((TOK, COLS), BF16),
            pltpu.VMEM((TOK, COLS), BF16),
            pltpu.VMEM((FEAT, TOK), BF16),
            pltpu.VMEM((32, ROWS, COLS), BF16),
            pltpu.VMEM((32, ROWS, FEAT), BF16),
            pltpu.VMEM((8, TOK, CH), BF16),
            pltpu.VMEM((8, 128, CH), BF16),
            pltpu.VMEM((8, 128, CH), BF16),
            pltpu.VMEM((8, 3, 32, CH), BF16),
            pltpu.VMEM((8, 32, CH), BF16),
            pltpu.VMEM((8, 32, CH), BF16),
            pltpu.VMEM((8, 32, CH), F32),
            pltpu.VMEM((TOK, R), BF16),
            pltpu.VMEM((4, TOK, CH), BF16),
            pltpu.VMEM((TOK, R), BF16),
            pltpu.VMEM((32, 128), F32),
            pltpu.VMEM((1, R), F32),
            pltpu.VMEM((TOK, 128), F32),
            pltpu.VMEM((1, R), F32),
            pltpu.VMEM((16, 1, SHARE), F32),
            pltpu.VMEM((31, 1, SHARE), F32),
            pltpu.VMEM((8, 1, SHARE), F32),
            dma((6,)), dma((8, 3)), dma, dma((16,)), dma, dma((8,)), dma, dma((9,)), dma,
            dma, dma((8,)), dma, dma((8,)), dma, dma((8,)),
            dma, dma((5,)), dma, dma((5,)), dma, dma, dma, dma,
        ],
        compiler_params=pltpu.CompilerParams(
            collective_id=0, has_side_effects=True, vmem_limit_bytes=62 * 2**20
        ),
    )(hidden.T, w_down.T, w_up, norm_gain, cotangent)
    return queries, dhidden.T, dgain.reshape(SHARE)


def solution(mesh):
    placed = (P("head", "lat"), P("lat", "head"), P("head", "lat"), P(), P("head", "lat"))
    return jax.shard_map(
        body,
        mesh=mesh,
        in_specs=placed,
        out_specs=(P("head", "lat"), P("head", "lat"), P("lat")),
        check_vma=False,
    )
```
